128 devices in a mesh: group: 8 (over x_lo, y), dev: 16 (over x_hi, z, core).
Axes of the slice: x: 4 (x_hi: 2, x_lo: 2; x = x_hi * 2 + x_lo), y: 4, z: 4, core: 2. Of those that a mesh axis runs over, the one named last changes fastest.
Arguments:
- x_act: bfloat16 [40960, 4608], P(('group', 'dev')), may hold values from -2 to 2
- cotangent: bfloat16 [40960, 1024], P(('group', 'dev')), may hold values from -0.5 to 0.5
- sign_bits: int32 [1024], replicated, may hold values from 0 to 1
Outputs:
- rotated_sum: bfloat16 [4608, 1024], P('dev', 'group')
- mean_grad: bfloat16 [4608, 1024], replicated
The draws below stay inside these ranges and needn't reach their ends.
All inputs are finite; a program needn't handle non-finite values.
Results may differ from the reference program's by a relative error of at most 0.001.
Values may be sent and summed in bfloat16 or wider, within the bound.
A program may use at most 128 MiB of HBM per device.

```python
import jax
import jax.numpy as jnp
from jax import lax

D = 4608
KVW = 1024
BLOCK = 128
TOK_DEV = 320
TOKENS = 40960
N_GROUP = 8
N_DEV = 16


def draw_x_act(key, part):
    key = jax.random.fold_in(key, 17)
    values = jax.random.randint(key, (TOKENS, D), -7, 8).astype(jnp.float32) / 8.0
    return values.astype(jnp.bfloat16)


def draw_cotangent(key, part):
    key = jax.random.fold_in(key, 29)
    values = jax.random.randint(key, (TOKENS, KVW), -7, 8).astype(jnp.float32) / 16.0
    return values.astype(jnp.bfloat16)


def with_ends(result, rng, least, high):
    longest = result.shape.index(max(result.shape))
    spots = []
    for shift in (0, 1):
        where = [jax.random.randint(jax.random.fold_in(rng, axis), (), 0, length) for axis, length in enumerate(result.shape)]
        where[longest] = (where[longest] + shift) % result.shape[longest]
        spots.append(tuple(where))
    return result.at[spots[0]].set(least).at[spots[1]].set(high)


def setup_inputs(seed: int = 0) -> dict:
    arg_keys = jax.random.split(jax.random.key(seed), 4)
    return {
        "x_act": draw_x_act(jax.random.fold_in(arg_keys[3], 71), 0),
        "cotangent": draw_cotangent(jax.random.fold_in(arg_keys[3], 71), 0),
        "sign_bits": with_ends(jax.random.randint(arg_keys[2], (KVW,), 0, 2), jax.random.fold_in(arg_keys[2], 1), 0, 1).astype(jnp.int32),
    }


def hadamard():
    index_vals = jnp.arange(BLOCK)
    both = jnp.bitwise_and(index_vals[:, None], index_vals[None, :])
    parity = jnp.zeros_like(both)
    for bit_pos in range(7):
        parity = parity + jnp.bitwise_and(jnp.right_shift(both, bit_pos), 1)
    return (1 - 2 * (parity % 2)).astype(jnp.float32)


def rotate(matrix, signs, hmat):
    rows = matrix.shape[0]
    blocks = (matrix * signs[None, :]).reshape(rows, -1, BLOCK)
    turned = jnp.einsum("rbi,ij->rbj", blocks, hmat, precision=lax.Precision.HIGHEST)
    return turned.reshape(rows, -1)


def unrotate(matrix, signs, hmat):
    rows = matrix.shape[0]
    blocks = matrix.reshape(rows, -1, BLOCK)
    turned = jnp.einsum("rbi,ij->rbj", blocks, hmat, precision=lax.Precision.HIGHEST)
    return (turned / BLOCK).reshape(rows, -1) * signs[None, :]


def quantize(matrix):
    shape = matrix.shape
    blocks = matrix.reshape(shape[:-1] + (shape[-1] // BLOCK, BLOCK))
    largest = jnp.max(jnp.abs(blocks), axis=-1)
    powers = jnp.asarray([2.0 ** k for k in range(-7, 31)], dtype=jnp.float32)
    exceeds = largest[..., None] > 63.5 * powers
    scales = jnp.max(jnp.where(exceeds, powers, 0.00390625), axis=-1).astype(jnp.bfloat16)
    ratio = blocks / scales.astype(jnp.float32)[..., None]
    floored = jnp.floor(ratio)
    fraction = ratio - floored
    odd_level = (floored - 2.0 * jnp.floor(0.5 * floored)) == 1.0
    round_up = (fraction > 0.5) | ((fraction == 0.5) & odd_level)
    levels = (floored + round_up.astype(jnp.float32)).astype(jnp.bfloat16)
    return levels.reshape(shape), scales


def dequant(levels, scales):
    shape = levels.shape
    blocks = levels.astype(jnp.float32).reshape(shape[:-1] + (shape[-1] // BLOCK, BLOCK))
    return (blocks * scales.astype(jnp.float32)[..., None]).reshape(shape)


def reference(x_act, cotangent, sign_bits):
    signs = (2 * sign_bits - 1).astype(jnp.float32)
    hmat = hadamard()
    parts = []
    for group_idx in range(N_GROUP):
        def add_device(dev_idx, total):
            start = ((group_idx * N_DEV + dev_idx) * TOK_DEV).astype(jnp.int32)
            x_rows = lax.dynamic_slice_in_dim(x_act, start, TOK_DEV, 0)
            g_rows = lax.dynamic_slice_in_dim(cotangent, start, TOK_DEV, 0)
            local = lax.dot_general(x_rows, g_rows, (((0,), (0,)), ((), ())), preferred_element_type=jnp.float32)
            levels, scales = quantize(rotate(local, signs, hmat))
            return total + dequant(levels, scales)
        group_total = lax.fori_loop(0, N_DEV, add_device, jnp.zeros((D, KVW), jnp.float32))
        parts.append(quantize(group_total))
    running = parts[0]
    for group_idx in range(1, N_GROUP):
        running = quantize(dequant(*running) + dequant(*parts[group_idx]))
    total = dequant(*running) / (N_GROUP * N_DEV)
    return total.astype(jnp.bfloat16), unrotate(total, signs, hmat).astype(jnp.bfloat16)
```

```python
import functools

import jax
import jax.numpy as jnp
from jax import lax
from jax.experimental import pallas as pl
from jax.experimental.pallas import tpu as pltpu
from jax.sharding import PartitionSpec as P

BLOCK = 128
TOK = 320
D = 4608
KVW = 1024
STAGES = 9
QUAD = 1152
OWN = 288
PART = 96
MAGIC = 12582912.0
MESH = pl.DeviceIdType.MESH


def hadamard_in_kernel():
    i = lax.broadcasted_iota(jnp.int32, (BLOCK, BLOCK), 0)
    j = lax.broadcasted_iota(jnp.int32, (BLOCK, BLOCK), 1)
    both = i & j
    parity = jnp.zeros_like(both)
    for bit in range(7):
        parity = parity + ((both >> bit) & 1)
    return (1 - 2 * (parity & 1)).astype(jnp.float32).astype(jnp.bfloat16)


def scale_of(largest):
    scale = jnp.full_like(largest, 2.0**-8)
    inv = jnp.full_like(largest, 2.0**8)
    for e in (32, 16, 8, 4, 2, 1):
        cand = scale * 2.0**e
        take = largest > cand * 63.5
        scale = jnp.where(take, cand, scale)
        inv = jnp.where(take, inv * 2.0**-e, inv)
    return jnp.minimum(scale, 2.0**30), jnp.maximum(inv, 2.0**-30)


def inverse_of(power):
    scale = jnp.full_like(power, 2.0**-8)
    inv = jnp.full_like(power, 2.0**8)
    for e in (32, 16, 8, 4, 2, 1):
        cand = scale * 2.0**e
        take = power >= cand
        scale = jnp.where(take, cand, scale)
        inv = jnp.where(take, inv * 2.0**-e, inv)
    return inv


def merge_meta(a, b):
    row = lax.broadcasted_iota(jnp.int32, a.shape, 0)
    return jnp.where(row < 2, jnp.minimum(a, b), a + b)


def wire_meta(m):
    unit, total = m[0:2], m[2:4]
    inv = inverse_of(unit)
    exact = total * inv * 127.0 <= 32767.0
    nan = jnp.full_like(unit, jnp.nan)
    zero = jnp.zeros((4, BLOCK), jnp.float32)
    return inv, jnp.concatenate([jnp.where(exact, unit, nan), jnp.where(exact, total, nan), zero], axis=0)


def kernel(
    x_ref, cot_ref, sb_ref, rot_ref, mean_ref,
    ct3, tmp, own, out_, got, om, sm, gm, acc, accm,
    zs, zsm, zr, zrm, xs, xsm, xr, xrm, gbuf, parts, mblk,
    sib_s, sib_r, z_s, z_r, x_s, x_r, g_s, g_r, a_s, a_r, f_s, f_r, l_s,
):
    g = lax.axis_index("group")
    d = lax.axis_index("dev")
    xl, y = g // 4, g % 4
    xh, z, c = d // 8, (d // 2) % 4, d % 2
    z_hi, k = z // 2, (z % 2) * 2 + c
    x = xh * 2 + xl

    def dev(xx, yy, zz, cc):
        return ((xx % 2) * 4 + yy, (xx // 2) * 8 + zz * 2 + cc)

    sibling = dev(x, y, z, 1 - c)
    partner = dev((x + 2) % 4, y, z, c)
    self_send = (k == g // 2).astype(jnp.int32)

    bar = pltpu.get_barrier_semaphore()

    def greet(who):
        pl.semaphore_signal(bar, inc=1, device_id=who, device_id_type=MESH)

    greet(sibling)
    for delta in (1, 2, 3):
        greet(dev((x + delta) % 4, y, z, c))
        greet(dev(x, (y + delta) % 4, z, c))
        greet(dev(x, y, (z + delta) % 4, c))
    ksrc = g // 2
    zsrc, csrc = z_hi * 2 + ksrc // 2, ksrc % 2
    for other in range(8):

        @pl.when(jnp.logical_or(self_send == 0, g != other))
        def _():
            greet((jnp.int32(other), xh * 8 + zsrc * 2 + csrc))

    hmat = hadamard_in_kernel()
    signs = (2 * sb_ref[...] - 1).astype(jnp.float32)
    for blk in range(8):
        cols = slice(blk * BLOCK, (blk + 1) * BLOCK)
        signed = (cot_ref[:, cols].astype(jnp.float32) * signs[:, cols]).astype(jnp.bfloat16)
        turned = lax.dot_general(hmat, signed, (((1,), (1,)), ((), ())), preferred_element_type=jnp.float32)
        hi = turned.astype(jnp.bfloat16)
        rest = turned - hi.astype(jnp.float32)
        mid = rest.astype(jnp.bfloat16)
        low = (rest - mid.astype(jnp.float32)).astype(jnp.bfloat16)
        kk, b = blk // 2, blk % 2
        r0 = (kk % 2) * 512 + (kk // 2) * 256 + b * BLOCK
        rows = slice(r0, r0 + BLOCK)
        for n, term in enumerate((hi, mid, low)):
            ct3[rows, n * 256 : (n + 1) * 256] = term[:, :256]
        ct3[rows, 768:896] = jnp.concatenate([hi[:, 256:], mid[:, 256:]], axis=1)
        ct3[rows, 896:1024] = jnp.concatenate([low[:, 256:], jnp.zeros((BLOCK, 64), jnp.bfloat16)], axis=1)

    def compute(s, core, lev, met):
        for X in (0, 1):
            lanes = [pl.ds(pl.multiple_of(X * 2304 + h * QUAD + s * BLOCK, BLOCK), BLOCK) for h in (0, 1)]
            xa = jnp.concatenate([x_ref[:, l] for l in lanes], axis=1)
            x3 = jnp.concatenate([xa[:256]] * 3 + [xa[256:]] * 3 + [jnp.zeros((64, 256), jnp.bfloat16)], axis=0)
            lhs = ct3[pl.ds(pl.multiple_of(core * 512, 512), 512), :]
            tmp[...] = jnp.dot(lhs, x3, preferred_element_type=jnp.float32)

            def sub(Z, b):
                return tmp[(Z % 2) * 256 + b * BLOCK : (Z % 2) * 256 + (b + 1) * BLOCK, (Z // 2) * BLOCK : (Z // 2 + 1) * BLOCK]

            largest = jnp.concatenate(
                [jnp.max(jnp.abs(sub(Z, b)), axis=0, keepdims=True) for Z in range(4) for b in range(2)], axis=0
            )
            scale, inv = scale_of(largest)
            for Z in range(4):
                for b in range(2):
                    r = Z * 2 + b
                    level = (sub(Z, b) * inv[r : r + 1] + MAGIC) - MAGIC
                    lev[s, X, Z, b * BLOCK : (b + 1) * BLOCK, :] = (level * scale[r : r + 1]).astype(jnp.bfloat16)
                mine = scale[2 * Z : 2 * Z + 2]
                met[s, X, Z] = jnp.concatenate([mine, mine, jnp.zeros((4, BLOCK), jnp.float32)], axis=0)

    def remote(src, dst, ss, rs, who):
        return pltpu.make_async_remote_copy(src, dst, ss, rs, device_id=who, device_id_type=MESH)

    def sib_copies(s):
        return (
            remote(out_.at[s], got.at[s], sib_s.at[s, 0], sib_r.at[s, 0], sibling),
            remote(sm.at[s], gm.at[s], sib_s.at[s, 1], sib_r.at[s, 1], sibling),
        )

    def z_copies_zfirst(s, dz):
        who = dev(x, y, (z + dz) % 4, c)
        i = dz - 1
        return (
            remote(zs.at[s, i], zr.at[s, i], z_s.at[s, i, 0], z_r.at[s, i, 0], who),
            remote(zsm.at[s, i], zrm.at[s, i], z_s.at[s, i, 1], z_r.at[s, i, 1], who),
        )

    def z_copies_xfirst(s, dz):
        who = dev(x, y, (z + dz) % 4, c)
        i = dz - 1
        return (
            remote(zs.at[s, i, 0], zr.at[s, i, 0], z_s.at[s, i, 0], z_r.at[s, i, 0], who),
            remote(zsm.at[s, i, 0], zrm.at[s, i, 0], z_s.at[s, i, 1], z_r.at[s, i, 1], who),
        )

    def x_copies_zfirst(s):
        return (
            remote(xs.at[s, 0], xr.at[s, 0], x_s.at[s, 0], x_r.at[s, 0], partner),
            remote(xsm.at[s, 0], xrm.at[s, 0], x_s.at[s, 1], x_r.at[s, 1], partner),
        )

    def x_copies_xfirst(s):
        return (
            remote(xs.at[s], xr.at[s], x_s.at[s, 0], x_r.at[s, 0], partner),
            remote(xsm.at[s], xrm.at[s], x_s.at[s, 1], x_r.at[s, 1], partner),
        )

    def g_copies(j, b):
        who = (2 * k + b, xh * 8 + (z_hi * 2 + j // 2) * 2 + j % 2)
        src = gbuf.at[b, pl.ds(pl.multiple_of(j * OWN, 32), OWN), :]
        return remote(src, parts.at[g], g_s.at[j, b], g_r.at[g], who)

    def start(copies):
        for copy in copies:
            copy.start()

    def arrive(copies):
        for copy in copies:
            copy.wait_recv()

    def left(copies):
        for copy in copies:
            copy.wait_send()

    def half(b):
        return slice(b * BLOCK, (b + 1) * BLOCK)

    def pair_block(s, X, Z, b):
        return own[s, X, Z, half(b), :].astype(jnp.float32) + got[s, X, Z, half(b), :].astype(jnp.float32)

    def encode(value, inv):
        return (value * inv).astype(jnp.int16)

    def decode(ref, index, b, meta):
        return ref[index + (half(b), slice(None))].astype(jnp.float32) * meta[b : b + 1]

    def pair(s):
        arrive(sib_copies(s))

        @pl.when(s % 2 == 1)
        def _():
            for X in (0, 1):
                for b in (0, 1):
                    acc[s, X, half(b), :] = pair_block(s, X, z, b)
                accm[s, X] = merge_meta(om[s, X, z], gm[s, X, z])
            for dz in (1, 2, 3):
                Z = (z + dz) % 4
                for X in (0, 1):
                    inv, meta = wire_meta(merge_meta(om[s, X, Z], gm[s, X, Z]))
                    zsm[s, dz - 1, X] = meta
                    for b in (0, 1):
                        zs[s, dz - 1, X, half(b), :] = encode(pair_block(s, X, Z, b), inv[b : b + 1])
                start(z_copies_zfirst(s, dz))

        @pl.when(s % 2 == 0)
        def _():
            for Z in range(4):
                inv, meta = wire_meta(merge_meta(om[s, 1 - xh, Z], gm[s, 1 - xh, Z]))
                xsm[s, Z] = meta
                for b in (0, 1):
                    xs[s, Z, half(b), :] = encode(pair_block(s, 1 - xh, Z, b), inv[b : b + 1])
            start(x_copies_xfirst(s))
            for Z in range(4):
                for b in (0, 1):
                    acc[s, Z, half(b), :] = pair_block(s, xh, Z, b)
                accm[s, Z] = merge_meta(om[s, xh, Z], gm[s, xh, Z])

    def second(s):
        @pl.when(s % 2 == 1)
        def _():
            for dz in (1, 2, 3):
                arrive(z_copies_zfirst(s, dz))
            other = 1 - xh
            metas = [zrm[s, i, other] for i in range(3)]
            inv, meta = wire_meta(functools.reduce(merge_meta, metas, accm[s, other]))
            xsm[s, 0] = meta
            for b in (0, 1):
                t = acc[s, other, half(b), :]
                for i in range(3):
                    t = t + decode(zr, (s, i, other), b, metas[i])
                xs[s, 0, half(b), :] = encode(t, inv[b : b + 1])
            start(x_copies_zfirst(s))
            metas = [zrm[s, i, xh] for i in range(3)]
            for b in (0, 1):
                t = acc[s, xh, half(b), :]
                for i in range(3):
                    t = t + decode(zr, (s, i, xh), b, metas[i])
                acc[s, xh, half(b), :] = t

        @pl.when(s % 2 == 0)
        def _():
            arrive(x_copies_xfirst(s))
            for dz in (1, 2, 3):
                Z = (z + dz) % 4
                arrived = xrm[s, Z]
                inv, meta = wire_meta(merge_meta(accm[s, Z], arrived))
                zsm[s, dz - 1, 0] = meta
                for b in (0, 1):
                    t = acc[s, Z, half(b), :] + decode(xr, (s, Z), b, arrived)
                    zs[s, dz - 1, 0, half(b), :] = encode(t, inv[b : b + 1])
                start(z_copies_xfirst(s, dz))
            arrived = xrm[s, z]
            for b in (0, 1):
                acc[s, z, half(b), :] = acc[s, z, half(b), :] + decode(xr, (s, z), b, arrived)

    def third(s):
        @pl.when(s % 2 == 1)
        def _():
            arrive(x_copies_zfirst(s))
            arrived = xrm[s, 0]
            for b in (0, 1):
                tmp[half(b), :BLOCK] = acc[s, xh, half(b), :] + decode(xr, (s, 0), b, arrived)

        @pl.when(s % 2 == 0)
        def _():
            for dz in (1, 2, 3):
                arrive(z_copies_xfirst(s, dz))
            metas = [zrm[s, i, 0] for i in range(3)]
            for b in (0, 1):
                t = acc[s, z, half(b), :]
                for i in range(3):
                    t = t + decode(zr, (s, i, 0), b, metas[i])
                tmp[half(b), :BLOCK] = t

        largest = jnp.concatenate(
            [jnp.max(jnp.abs(tmp[half(b), :BLOCK]), axis=0, keepdims=True) for b in (0, 1)], axis=0
        )
        scale, inv = scale_of(largest)
        for b in (0, 1):
            level = (tmp[half(b), :BLOCK] * inv[b : b + 1] + MAGIC) - MAGIC
            value = level * scale[b : b + 1]
            gbuf[b, pl.ds(pl.multiple_of(s * BLOCK, BLOCK), BLOCK), :] = value.T.astype(jnp.bfloat16)

        @pl.when(jnp.logical_and(s >= 2, s % 2 == 0))
        def _():
            j = s // 2 - 1
            for b in (0, 1):
                to_self = jnp.logical_and(j == k, 2 * k + b == g)

                @pl.when(to_self)
                def _():
                    parts[g] = gbuf[b, pl.ds(pl.multiple_of(j * OWN, 32), OWN), :]

                @pl.when(jnp.logical_not(to_self))
                def _():
                    g_copies(j, b).start()

    def first_loop(s, _):
        @pl.when(s < STAGES)
        def _():
            compute(s, 1 - c, out_, sm)

            @pl.when(s == 0)
            def _():
                pl.semaphore_wait(bar, 18 - self_send)

            start(sib_copies(s))
            compute(s, c, own, om)

        @pl.when(s >= 1)
        def _():
            pair(s - 1)

        return 0

    lax.fori_loop(0, STAGES + 1, first_loop, 0)

    LAG = 2

    def second_loop(t, _):
        @pl.when(t < STAGES)
        def _():
            second(t)

        @pl.when(t >= LAG)
        def _():
            third(t - LAG)

        return 0

    lax.fori_loop(0, STAGES + LAG, second_loop, 0)

    def await_part(other):
        src = gbuf.at[0, pl.ds(0, OWN), :]

        @pl.when(jnp.logical_or(self_send == 0, g != other))
        def _():
            remote(src, parts.at[other], g_s.at[0, 0], g_r.at[other], sibling).wait_recv()

    await_part(0)
    total = parts[0].astype(jnp.float32)
    for other in range(1, 8):
        await_part(other)
        total = total + parts[other].astype(jnp.float32)
        scale, inv = scale_of(jnp.max(jnp.abs(total), axis=1, keepdims=True))
        total = ((total * inv + MAGIC) - MAGIC) * scale
    total = total * (1.0 / 128.0)
    rot_ref[...] = total.astype(jnp.bfloat16)
    turned = jnp.dot(total.astype(jnp.bfloat16), hmat, preferred_element_type=jnp.float32)
    my_signs = (2 * sb_ref[:, pl.ds(pl.multiple_of(g * BLOCK, BLOCK), BLOCK)] - 1).astype(jnp.float32)
    mean = turned * (1.0 / BLOCK) * my_signs
    bad = jnp.max(jnp.where(mean == mean, 0.0, 1.0), axis=(0, 1), keepdims=True)
    mean = jnp.where(bad > 0.0, jnp.nan, mean)
    mblk[...] = mean.astype(jnp.bfloat16)

    order = ("xyz", "yzx", "zxy")

    def rows(p):
        return pl.ds(p * PART, PART)

    def slabs(p, phase, xx, yy, zz):
        hh, ll = xx // 2, xx % 2
        if phase == 0:
            cols = pl.ds(pl.multiple_of((ll * 4 + yy) * BLOCK, BLOCK), BLOCK)
            return [mean_ref.at[hh, zz, c, rows(p), cols]]
        quarter = [pl.ds(pl.multiple_of(l * 512 + yy * BLOCK, BLOCK), BLOCK) for l in (0, 1)]
        whole_l = pl.ds(pl.multiple_of(ll * 512, 512), 512)
        if p == 0:
            if phase == 1:
                return [mean_ref.at[:, zz, c, rows(p), q] for q in quarter]
            return [mean_ref.at[:, zz, c, rows(p), :]]
        if p == 1:
            if phase == 1:
                return [mean_ref.at[hh, zz, c, rows(p), whole_l]]
            return [mean_ref.at[hh, :, c, rows(p), whole_l]]
        if phase == 1:
            cols = pl.ds(pl.multiple_of((ll * 4 + yy) * BLOCK, BLOCK), BLOCK)
            return [mean_ref.at[hh, :, c, rows(p), cols]]
        return [mean_ref.at[:, :, c, rows(p), q] for q in quarter]

    def moved(axis, delta):
        return (
            (x + delta) % 4 if axis == "x" else x,
            (y + delta) % 4 if axis == "y" else y,
            (z + delta) % 4 if axis == "z" else z,
        )

    def gather_sends(p, phase, delta):
        to = moved(order[p][phase], delta)
        mine = slabs(p, phase, x, y, z)
        src = [mblk.at[rows(p), :]] if phase == 0 else mine
        return [
            remote(a, b, a_s.at[p, phase, delta - 1, i], a_r.at[p, phase, delta - 1, i], dev(*to, c))
            for i, (a, b) in enumerate(zip(src, mine))
        ]

    def gather_gets(p, phase, delta):
        at = moved(order[p][phase], 4 - delta)
        return [
            remote(a, a, a_s.at[p, phase, delta - 1, i], a_r.at[p, phase, delta - 1, i], sibling)
            for i, a in enumerate(slabs(p, phase, *at))
        ]

    def forwards(p, n):
        at = (x, y, z) if n == 0 else moved(order[p][2], 4 - n)
        return [
            remote(a, a, f_s.at[p, n, i], f_r.at[p, n, i], sibling) for i, a in enumerate(slabs(p, 2, *at))
        ]

    def forwarded(p, n):
        at = (x, y, z) if n == 0 else moved(order[p][2], 4 - n)
        out = []
        hh, ll = at[0] // 2, at[0] % 2
        quarter = [pl.ds(pl.multiple_of(l * 512 + at[1] * BLOCK, BLOCK), BLOCK) for l in (0, 1)]
        whole_l = pl.ds(pl.multiple_of(ll * 512, 512), 512)
        if p == 0:
            refs = [mean_ref.at[:, at[2], 1 - c, rows(p), :]]
        elif p == 1:
            refs = [mean_ref.at[hh, :, 1 - c, rows(p), whole_l]]
        else:
            refs = [mean_ref.at[:, :, 1 - c, rows(p), q] for q in quarter]
        for i, a in enumerate(refs):
            out.append(remote(a, a, f_s.at[p, n, i], f_r.at[p, n, i], sibling))
        return out

    home = mean_ref.at[xh, z, c, :, pl.ds(pl.multiple_of(g * BLOCK, BLOCK), BLOCK)]
    keep = pltpu.make_async_copy(mblk, home, l_s)
    keep.start()
    for p in range(3):
        for delta in (1, 3, 2):
            start(gather_sends(p, 0, delta))
    keep.wait()
    for phase in (1, 2):
        for p in range(3):
            for delta in (1, 3, 2):
                arrive(gather_gets(p, phase - 1, delta))
            for delta in (1, 3, 2):
                start(gather_sends(p, phase, delta))
            if phase == 2:
                start(forwards(p, 0))
    for delta in (1, 3, 2):
        for p in range(3):
            arrive(gather_gets(p, 2, delta))
            start(forwards(p, delta))

    for p in range(3):
        for n in (0, 1, 3, 2):
            arrive(forwarded(p, n))
    for p in range(3):
        for n in range(4):
            left(forwards(p, n))
        for phase in range(3):
            for delta in (1, 2, 3):
                left(gather_sends(p, phase, delta))

    def drain(s, _):
        left(sib_copies(s))

        @pl.when(s % 2 == 1)
        def _():
            for dz in (1, 2, 3):
                left(z_copies_zfirst(s, dz))
            left(x_copies_zfirst(s))

        @pl.when(s % 2 == 0)
        def _():
            for dz in (1, 2, 3):
                left(z_copies_xfirst(s, dz))
            left(x_copies_xfirst(s))

        return 0

    lax.fori_loop(0, STAGES, drain, 0)

    def drain_g(j, _):
        for b in (0, 1):

            @pl.when(jnp.logical_not(jnp.logical_and(j == k, 2 * k + b == g)))
            def _():
                g_copies(j, b).wait_send()

        return 0

    lax.fori_loop(0, 4, drain_g, 0)


def fast(x_act, cotangent, sign_bits):
    bf16, f32, i16 = jnp.bfloat16, jnp.float32, jnp.int16
    dma = pltpu.SemaphoreType.DMA
    vmem = pltpu.VMEM
    rotated, mean = pl.pallas_call(
        kernel,
        out_shape=(
            jax.ShapeDtypeStruct((OWN, BLOCK), bf16),
            jax.ShapeDtypeStruct((2, 4, 2, OWN, KVW), bf16),
        ),
        in_specs=[pl.BlockSpec(memory_space=vmem)] * 3,
        out_specs=(pl.BlockSpec(memory_space=vmem), pl.BlockSpec(memory_space=pl.ANY)),
        scratch_shapes=[
            vmem((KVW, KVW), bf16),
            vmem((512, 256), f32),
            vmem((STAGES, 2, 4, 256, BLOCK), bf16),
            vmem((STAGES, 2, 4, 256, BLOCK), bf16),
            vmem((STAGES, 2, 4, 256, BLOCK), bf16),
            vmem((STAGES, 2, 4, 8, BLOCK), f32),
            vmem((STAGES, 2, 4, 8, BLOCK), f32),
            vmem((STAGES, 2, 4, 8, BLOCK), f32),
            vmem((STAGES, 4, 256, BLOCK), f32),
            vmem((STAGES, 4, 8, BLOCK), f32),
            vmem((STAGES, 3, 2, 256, BLOCK), i16),
            vmem((STAGES, 3, 2, 8, BLOCK), f32),
            vmem((STAGES, 3, 2, 256, BLOCK), i16),
            vmem((STAGES, 3, 2, 8, BLOCK), f32),
            vmem((STAGES, 4, 256, BLOCK), i16),
            vmem((STAGES, 4, 8, BLOCK), f32),
            vmem((STAGES, 4, 256, BLOCK), i16),
            vmem((STAGES, 4, 8, BLOCK), f32),
            vmem((2, QUAD, BLOCK), bf16),
            vmem((8, OWN, BLOCK), bf16),
            vmem((OWN, BLOCK), bf16),
            dma((STAGES, 2)), dma((STAGES, 2)),
            dma((STAGES, 3, 2)), dma((STAGES, 3, 2)),
            dma((STAGES, 2)), dma((STAGES, 2)),
            dma((4, 2)), dma((8,)),
            dma((3, 3, 3, 2)), dma((3, 3, 3, 2)),
            dma((3, 4, 2)), dma((3, 4, 2)),
            dma,
        ],
        compiler_params=pltpu.CompilerParams(
            collective_id=0, has_side_effects=True, vmem_limit_bytes=60 * 2**20
        ),
        cost_estimate=pl.CostEstimate(flops=10**10, bytes_accessed=3 * 10**7, transcendentals=0),
        name="sync",
    )(x_act, cotangent, sign_bits.reshape(1, KVW))
    return rotated, mean


def passed_along(value, axis, steps):
    count = lax.axis_size(axis)
    leading, last = (max(0, -steps), min(count, count - steps))
    return lax.ppermute(value, axis, [(source, source + steps) for source in range(leading, last)])


def from_root(x, axis, root):
    mine = lax.axis_index(axis) == root
    return lax.psum(jnp.where(mine, x, jnp.zeros_like(x)), axis)


def hadamard():
    index_vals = jnp.arange(BLOCK)
    both = jnp.bitwise_and(index_vals[:, None], index_vals[None, :])
    parity = jnp.zeros_like(both)
    for bit_pos in range(7):
        parity = parity + jnp.bitwise_and(jnp.right_shift(both, bit_pos), 1)
    return (1 - 2 * (parity % 2)).astype(jnp.float32)


def rotate(matrix, signs, hmat):
    rows = matrix.shape[0]
    blocks = (matrix * signs[None, :]).reshape(rows, -1, BLOCK)
    turned = jnp.einsum("rbi,ij->rbj", blocks, hmat, precision=lax.Precision.HIGHEST)
    return turned.reshape(rows, -1)


def unrotate(matrix, signs, hmat):
    rows = matrix.shape[0]
    blocks = matrix.reshape(rows, -1, BLOCK)
    turned = jnp.einsum("rbi,ij->rbj", blocks, hmat, precision=lax.Precision.HIGHEST)
    return (turned / BLOCK).reshape(rows, -1) * signs[None, :]


def quantize(matrix):
    shape = matrix.shape
    blocks = matrix.reshape(shape[:-1] + (shape[-1] // BLOCK, BLOCK))
    largest = jnp.max(jnp.abs(blocks), axis=-1)
    powers = jnp.asarray([2.0**k for k in range(-7, 31)], dtype=jnp.float32)
    exceeds = largest[..., None] > 63.5 * powers
    scales = jnp.max(jnp.where(exceeds, powers, 0.00390625), axis=-1).astype(jnp.bfloat16)
    ratio = blocks / scales.astype(jnp.float32)[..., None]
    floored = jnp.floor(ratio)
    fraction = ratio - floored
    odd_level = floored - 2.0 * jnp.floor(0.5 * floored) == 1.0
    round_up = (fraction > 0.5) | (fraction == 0.5) & odd_level
    levels = (floored + round_up.astype(jnp.float32)).astype(jnp.bfloat16)
    return (levels.reshape(shape), scales)


def dequant(levels, scales):
    shape = levels.shape
    blocks = levels.astype(jnp.float32).reshape(shape[:-1] + (shape[-1] // BLOCK, BLOCK))
    return (blocks * scales.astype(jnp.float32)[..., None]).reshape(shape)


def general(x_act, cotangent, sign_bits):
    signs = (2 * sign_bits - 1).astype(jnp.float32)
    hmat = hadamard()
    local = lax.dot_general(
        x_act, cotangent, (((0,), (0,)), ((), ())), preferred_element_type=jnp.float32
    )
    levels, scales = quantize(rotate(local, signs, hmat))
    width = levels.shape[1]
    members = lax.axis_size("dev")
    groups = lax.axis_size("group")
    rows = levels.shape[0] // members
    got_levels, got_scales = (
        lax.all_to_all(
            levels.reshape(members, rows, width), "dev", split_axis=0, concat_axis=0, tiled=True
        ),
        lax.all_to_all(
            scales.reshape(members, rows, width // BLOCK),
            "dev",
            split_axis=0,
            concat_axis=0,
            tiled=True,
        ),
    )
    group_total = jnp.sum(dequant(got_levels, got_scales), axis=0)
    own = quantize(group_total)
    position = lax.axis_index("group")

    def one_hop(step_idx, carry):
        arrived = passed_along((carry[0], carry[1]), "group", 1)
        merged = quantize(dequant(*arrived) + dequant(*own))
        chosen = position == step_idx
        return (jnp.where(chosen, merged[0], carry[0]), jnp.where(chosen, merged[1], carry[1]))

    running = lax.fori_loop(1, groups, one_hop, own)
    final = (from_root(running[0], "group", groups - 1), from_root(running[1], "group", groups - 1))
    total = dequant(*final) / (groups * members)
    column_share = width // groups
    own_columns = lax.dynamic_slice_in_dim(total, position * column_share, column_share, 1)
    rotated_sum = own_columns.astype(jnp.bfloat16)
    all_levels, all_scales = (
        lax.all_gather(final[0], "dev", axis=0, tiled=True),
        lax.all_gather(final[1], "dev", axis=0, tiled=True),
    )
    everything = dequant(all_levels, all_scales) / (groups * members)
    mean_grad = unrotate(everything, signs, hmat).astype(jnp.bfloat16)
    return (rotated_sum, mean_grad)


def body(x_act, cotangent, sign_bits):
    rotated, mean = fast(x_act, cotangent, sign_bits)
    marks = mean[:, :, :, 0, ::BLOCK].astype(jnp.float32)
    inexact = jnp.any(marks != marks)
    return lax.cond(
        inexact,
        lambda r, m: general(x_act, cotangent, sign_bits),
        lambda r, m: (r, m),
        rotated,
        mean.reshape(D, KVW),
    )


def solution(mesh):
    placed = (P(("group", "dev"), None), P(("group", "dev"), None), P())
    return jax.shard_map(
        body, mesh=mesh, in_specs=placed, out_specs=(P("dev", "group"), P()), check_vma=False
    )
```

```python
import functools

import jax
import jax.numpy as jnp
from jax import lax
from jax.experimental import pallas as pl
from jax.experimental.pallas import tpu as pltpu
from jax.sharding import PartitionSpec as P

BLOCK = 128
TOK = 320
D = 4608
KVW = 1024
STAGES = 9
QUAD = 1152
OWN = 288
PART = 96
SHARE = 32
LAG_A, LAG_B, LAG_C, LAG_D = 1, 5, 8, 10
MAGIC = 12582912.0
MESH = pl.DeviceIdType.MESH


def hadamard_in_kernel():
    i = lax.broadcasted_iota(jnp.int32, (BLOCK, BLOCK), 0)
    j = lax.broadcasted_iota(jnp.int32, (BLOCK, BLOCK), 1)
    both = i & j
    parity = jnp.zeros_like(both)
    for bit in range(7):
        parity = parity + ((both >> bit) & 1)
    return (1 - 2 * (parity & 1)).astype(jnp.float32).astype(jnp.bfloat16)


def scale_of(largest):
    scale = jnp.full_like(largest, 2.0**-8)
    for e in (32, 16, 8, 4, 2, 1):
        cand = scale * 2.0**e
        scale = jnp.where(largest > cand * 63.5, cand, scale)
    return jnp.minimum(scale, 2.0**30)


def rounded(value, scale):
    shift = scale * MAGIC
    return (value + shift) - shift


def inverse_of(power):
    scale = jnp.full_like(power, 2.0**-8)
    inv = jnp.full_like(power, 2.0**8)
    for e in (32, 16, 8, 4, 2, 1):
        cand = scale * 2.0**e
        take = power >= cand
        scale = jnp.where(take, cand, scale)
        inv = jnp.where(take, inv * 2.0**-e, inv)
    return inv


def on_wire(unit, total):
    inv = inverse_of(unit)
    exact = total * inv * 127.0 <= 32767.0
    return inv, jnp.where(exact, unit, jnp.nan), jnp.where(exact, total, jnp.nan)


def kernel(
    x_hbm, cot_ref, sb_ref, rot_ref, gat, bad_ref,
    xv, ct3, tmp0, tmp1, tmp2, tmp3, own, out_, got, om, sm, gm, pw, acc, accm,
    z1, z1m, z1r, z1rm, z2, z2m, z2r, z2rm, xs, xsm, xr, xrm, gbuf, parts, rbuf, rgot, gauge,
    sib_s, sib_r, z1_s, z1_r, z2_s, z2_r, x_s, x_r, g_s, g_r, r_s, r_r, a_s, a_r, f_r, l_s,
):
    g = lax.axis_index("group")
    d = lax.axis_index("dev")
    div, rem = (lambda a, b: lax.div(a, jnp.int32(b))), (lambda a, b: lax.rem(a, jnp.int32(b)))
    xl, y = div(g, 4), rem(g, 4)
    xh, z, c = div(d, 8), rem(div(d, 2), 4), rem(d, 2)
    z_hi, k = div(z, 2), rem(z, 2) * 2 + c
    x = xh * 2 + xl

    def dev(xx, yy, zz, cc):
        return (rem(xx, 2) * 4 + yy, div(xx, 2) * 8 + zz * 2 + cc)

    sibling = dev(x, y, z, 1 - c)
    partner = dev((x + 2) % 4, y, z, c)
    beside = (dev(x, y, (z + 1) % 4, c), dev(x, y, (z + 3) % 4, c))
    column = 2 * k + g // 4
    to_self = jnp.logical_and(k == g // 2, g % 2 == g // 4).astype(jnp.int32)

    fetch = pltpu.make_async_copy(x_hbm, xv, l_s)
    fetch.start()

    bar = pltpu.get_barrier_semaphore()

    def greet(who):
        pl.semaphore_signal(bar, inc=1, device_id=who, device_id_type=MESH)

    greet(sibling)
    for delta in (1, 2, 3):
        greet(dev((x + delta) % 4, y, z, c))
        greet(dev(x, (y + delta) % 4, z, c))
        greet(dev(x, y, (z + delta) % 4, c))
    for delta in (1, 2, 3):
        greet(dev(xh * 2 + 1 - xl, (y + delta) % 4, z, c))
    ksrc = g // 2
    for m in range(4):

        @pl.when(jnp.logical_or(to_self == 0, m != g % 4))
        def _():
            greet(((g % 2) * 4 + m, xh * 8 + (z_hi * 2 + ksrc // 2) * 2 + ksrc % 2))

    hmat = hadamard_in_kernel()
    signs = (2 * sb_ref[...] - 1).astype(jnp.float32)
    for blk in range(8):
        cols = slice(blk * BLOCK, (blk + 1) * BLOCK)
        signed = (cot_ref[:, cols].astype(jnp.float32) * signs[:, cols]).astype(jnp.bfloat16)
        turned = lax.dot_general(hmat, signed, (((1,), (1,)), ((), ())), preferred_element_type=jnp.float32)
        hi = turned.astype(jnp.bfloat16)
        rest = turned - hi.astype(jnp.float32)
        mid = rest.astype(jnp.bfloat16)
        low = (rest - mid.astype(jnp.float32)).astype(jnp.bfloat16)
        kk, b = blk // 2, blk % 2
        r0 = (kk % 2) * 512 + (kk // 2) * 256 + b * BLOCK
        rows = slice(r0, r0 + BLOCK)
        for n, term in enumerate((hi, mid, low)):
            ct3[rows, n * 256 : (n + 1) * 256] = term[:, :256]
        ct3[rows, 768:896] = jnp.concatenate([hi[:, 256:], mid[:, 256:]], axis=1)
        ct3[rows, 896:1024] = jnp.concatenate([low[:, 256:], jnp.zeros((BLOCK, 64), jnp.bfloat16)], axis=1)

    def product(s, core, X, tmp):
        lanes = [pl.ds(pl.multiple_of(X * 2304 + h * QUAD + s * BLOCK, BLOCK), BLOCK) for h in (0, 1)]
        xa = jnp.concatenate([xv[:, l] for l in lanes], axis=1)
        x3 = jnp.concatenate([xa[:256]] * 3 + [xa[256:]] * 3 + [jnp.zeros((64, 256), jnp.bfloat16)], axis=0)
        lhs = ct3[pl.ds(pl.multiple_of(core * 512, 512), 512), :]
        tmp[...] = jnp.dot(lhs, x3, preferred_element_type=jnp.float32)

    def quantized(s, X, tmp, lev, met):
        def sub(Z, b):
            r0, l0 = (Z % 2) * 256 + b * BLOCK, (Z // 2) * BLOCK
            return tmp[r0 : r0 + BLOCK, l0 : l0 + BLOCK]

        largest = jnp.concatenate(
            [jnp.max(jnp.abs(sub(Z, b)), axis=0, keepdims=True) for Z in range(4) for b in range(2)], axis=0
        )
        scale = scale_of(largest)
        met[s, X] = scale
        for Z in range(4):
            for b in range(2):
                r = Z * 2 + b
                lev[s, X, Z, half(b), :] = rounded(sub(Z, b), scale[r : r + 1]).astype(jnp.bfloat16)

    def half(b):
        return slice(b * BLOCK, (b + 1) * BLOCK)

    def remote(src, dst, ss, rs, who):
        return pltpu.make_async_remote_copy(src, dst, ss, rs, device_id=who, device_id_type=MESH)

    def both(src, srcm, dst, dstm, ss, n, rs, who):
        return (remote(src, dst, ss.at[2 * n], rs, who), remote(srcm, dstm, ss.at[2 * n + 1], rs, who))

    def sib_copies(s):
        return both(out_.at[s], sm.at[s], got.at[s], gm.at[s], sib_s, 0, sib_r.at[s], sibling)

    def z1_copies(s, way, n):
        a, b = z1.at[s, way], z1r.at[s, way]
        if n == 1:
            a, b = a.at[0], b.at[0]
        return both(a, z1m.at[s, way], b, z1rm.at[s, way], z1_s, n - 1, z1_r.at[s, way], beside[way])

    def z2_copies(s, way, n):
        a, b = z2.at[s, way], z2r.at[s, way]
        if n == 1:
            a, b = a.at[0], b.at[0]
        return both(a, z2m.at[s, way], b, z2rm.at[s, way], z2_s, n - 1, z2_r.at[s, way], beside[way])

    def x_copies(s, n):
        a, am, b, bm = xs.at[s], xsm.at[s], xr.at[s], xrm.at[s]
        if n == 1:
            a, am, b, bm = a.at[0], am.at[0], b.at[0], bm.at[0]
        return both(a, am, b, bm, x_s, 0 if n == 1 else 1, x_r.at[s], partner)

    def took(sem, rows):
        ref = gauge.at[pl.ds(0, rows), :]
        pltpu.make_async_copy(ref, ref, sem).wait()

    def g_copy(p, q):
        to = rem(g + q, 8)
        three = pl.ds(pl.multiple_of(p * PART, PART), PART)
        return remote(gbuf.at[to, three, :], parts.at[g, three, :], g_s, g_r.at[p], (to, d))

    def r_copy(s):
        t = 4 * s + rem(g, 4)
        j = div(t, 9)
        src = rbuf.at[pl.ds(pl.multiple_of(s * SHARE, SHARE), SHARE), :]
        dst = rgot.at[pl.ds(pl.multiple_of(rem(t, 9) * SHARE, SHARE), SHARE), :]
        who = (column, xh * 8 + (z_hi * 2 + div(j, 2)) * 2 + rem(j, 2))
        return remote(src, dst, r_s.at[s], r_r.at[rem(t, 9)], who), jnp.logical_and(to_self == 1, j == k), t

    def start(copies):
        for copy in copies:
            copy.start()

    def encode(value, inv):
        return (value * inv).astype(jnp.int16)

    def pair_block(s, X, Z, b):
        return own[s, X, Z, half(b), :].astype(jnp.float32) + got[s, X, Z, half(b), :].astype(jnp.float32)

    def add(s, i, b, block, unit, total):
        acc[s, i, half(b), :] = acc[s, i, half(b), :] + block.astype(jnp.float32) * unit
        accm[s, i, b : b + 1, :] = jnp.minimum(accm[s, i, b : b + 1, :], unit)
        accm[s, i, 2 + b : 3 + b, :] = accm[s, i, 2 + b : 3 + b, :] + total

    def packed(s, i, b):
        inv, unit, total = on_wire(accm[s, i, b : b + 1, :], accm[s, i, 2 + b : 3 + b, :])
        return encode(acc[s, i, half(b), :], inv), unit, total

    def z1_from_sums(s):
        two = (z + 2) % 4
        for way, (near, b) in enumerate((((z + 1) % 4, 1), ((z + 3) % 4, 0))):
            for kind, (i, bb) in enumerate(((near, b), (two, 1 - b))):
                block, unit, total = packed(s, i, bb)
                z1[s, way, 0, kind] = block
                z1m[s, way, kind : kind + 1, :] = unit
                z1m[s, way, 2 + kind : 3 + kind, :] = total
            start(z1_copies(s, way, 1))

    def z1_take(s, n, mine, right, left_):
        for way in (0, 1):
            took(z1_r.at[s, way], 256 * n + 16)
            for i in range(n):
                r = 4 * i
                b = way
                on = right(i) if way == 0 else left_(i)
                add(s, on, b, z1r[s, way, i, 1], z1rm[s, way, r + 1 : r + 2, :], z1rm[s, way, r + 3 : r + 4, :])
                block, unit, total = packed(s, on, b)
                z2[s, way, i] = block
                z2m[s, way, i : i + 1, :] = unit
                z2m[s, way, 2 + i : 3 + i, :] = total
            start(z2_copies(s, way, n))
            for i in range(n):
                r = 4 * i
                add(s, mine(i), 1 - way, z1r[s, way, i, 0], z1rm[s, way, r : r + 1, :], z1rm[s, way, r + 2 : r + 3, :])

    def z2_take(s, n, mine):
        for way in (0, 1):
            took(z2_r.at[s, way], 128 * n + 16)
            for i in range(n):
                add(s, mine(i), way, z2r[s, way, i], z2rm[s, way, i : i + 1, :], z2rm[s, way, 2 + i : 3 + i, :])

    def along_z_first(s):
        return rem(s, 3) != 1

    def step_a(s):
        took(sib_r.at[s], 2080)
        for X in (0, 1):
            unit = jnp.minimum(om[s, X], gm[s, X])
            total = om[s, X] + gm[s, X]
            inv, wire_unit, wire_total = on_wire(unit, total)
            for n, v in enumerate((unit, total, inv, wire_unit, wire_total)):
                pw[X, n] = v

        def row(X, n, Z, b):
            return pw[X, n, pl.ds(2 * Z + b, 1), :]

        def keep(i, ii, X, Z, b):
            acc[s, i, half(ii), :] = pair_block(s, X, Z, b)
            accm[s, i, ii : ii + 1, :] = row(X, 0, Z, b)
            accm[s, i, 2 + ii : 3 + ii, :] = row(X, 1, Z, b)

        @pl.when(along_z_first(s))
        def _():
            two, after, before = (z + 2) % 4, (z + 1) % 4, (z + 3) % 4
            for way, (near, b) in enumerate(((after, 1), (before, 0))):
                for X in (0, 1):
                    for kind, (Z, bb) in enumerate(((near, b), (two, 1 - b))):
                        z1[s, way, X, kind] = encode(pair_block(s, X, Z, bb), row(X, 2, Z, bb))
                        z1m[s, way, 4 * X + kind : 4 * X + kind + 1, :] = row(X, 3, Z, bb)
                        z1m[s, way, 4 * X + 2 + kind : 4 * X + 3 + kind, :] = row(X, 4, Z, bb)
                start(z1_copies(s, way, 2))
            for X in (0, 1):
                for b in (0, 1):
                    keep(X, b, X, z, b)
                keep(2 + X, 0, X, after, 0)
                keep(2 + X, 1, X, before, 1)

        @pl.when(jnp.logical_not(along_z_first(s)))
        def _():
            for Z in range(4):
                for b in (0, 1):
                    xs[s, Z, half(b), :] = encode(pair_block(s, 1 - xh, Z, b), row(1 - xh, 2, Z, b))
                    xsm[s, Z, b : b + 1, :] = row(1 - xh, 3, Z, b)
                    xsm[s, Z, 2 + b : 3 + b, :] = row(1 - xh, 4, Z, b)
            start(x_copies(s, 4))
            for Z in range(4):
                for b in (0, 1):
                    keep(Z, b, xh, Z, b)

    def x_take(s, i, n):
        for b in (0, 1):
            add(s, i, b, xr[s, n, half(b), :], xrm[s, n, b : b + 1, :], xrm[s, n, 2 + b : 3 + b, :])

    def step_b(s):
        @pl.when(along_z_first(s))
        def _():
            z1_take(s, 2, lambda i: i, lambda i: 2 + i, lambda i: 2 + i)

        @pl.when(jnp.logical_not(along_z_first(s)))
        def _():
            took(x_r.at[s], 1088)
            for Z in range(4):
                x_take(s, Z, Z)
            z1_from_sums(s)

    def step_c(s):
        @pl.when(along_z_first(s))
        def _():
            z2_take(s, 2, lambda i: i)
            for b in (0, 1):
                block, unit, total = packed(s, 1 - xh, b)
                xs[s, 0, half(b), :] = block
                xsm[s, 0, b : b + 1, :] = unit
                xsm[s, 0, 2 + b : 3 + b, :] = total
            start(x_copies(s, 1))

        @pl.when(jnp.logical_not(along_z_first(s)))
        def _():
            z1_take(s, 1, lambda i: z, lambda i: (z + 1) % 4, lambda i: (z + 3) % 4)

    def step_d(s):
        @pl.when(along_z_first(s))
        def _():
            took(x_r.at[s], 272)
            x_take(s, xh, 0)

        @pl.when(jnp.logical_not(along_z_first(s)))
        def _():
            z2_take(s, 1, lambda i: z)

        i = jnp.where(along_z_first(s), xh, z)
        sums = [acc[s, i, half(b), :] for b in (0, 1)]
        largest = jnp.concatenate([jnp.max(jnp.abs(t), axis=0, keepdims=True) for t in sums], axis=0)
        scale = scale_of(largest)
        for b in (0, 1):
            value = rounded(sums[b], scale[b : b + 1])
            value = value.T.astype(jnp.bfloat16)
            for m in range(4):
                gbuf[4 * b + m, pl.ds(pl.multiple_of(s * SHARE, SHARE), SHARE), :] = value[m * SHARE : (m + 1) * SHARE]

        @pl.when(rem(s, 3) == 2)
        def _():
            for q in range(1, 8):
                g_copy(div(s, 3), q).start()

    fetch.wait()

    def loop(t, _):
        @pl.when(t < STAGES)
        def _():
            product(t, 1 - c, 0, tmp0)
            product(t, 1 - c, 1, tmp1)
            quantized(t, 0, tmp0, out_, sm)
            product(t, c, 0, tmp2)
            quantized(t, 1, tmp1, out_, sm)
            product(t, c, 1, tmp3)

            @pl.when(t == 0)
            def _():
                pl.semaphore_wait(bar, 17 - to_self)

            start(sib_copies(t))
            quantized(t, 0, tmp2, own, om)
            quantized(t, 1, tmp3, own, om)

        for lag, step in ((LAG_A, step_a), (LAG_B, step_b), (LAG_C, step_c), (LAG_D, step_d)):

            @pl.when(jnp.logical_and(t >= lag, t < STAGES + lag))
            def _():
                step(t - lag)

        return 0

    lax.fori_loop(0, STAGES + LAG_D, loop, 0)

    parts[g] = gbuf[g]
    for p in range(3):
        took(g_r.at[p], 7 * PART)
    total = parts[0].astype(jnp.float32)
    for other in range(1, 8):
        total = total + parts[other].astype(jnp.float32)
        total = rounded(total, scale_of(jnp.max(jnp.abs(total), axis=1, keepdims=True)))
    total = total * (1.0 / 128.0)
    rbuf[...] = total.astype(jnp.bfloat16)
    turned = jnp.dot(total.astype(jnp.bfloat16), hmat, preferred_element_type=jnp.float32)
    my_signs = (2 * sb_ref[:, pl.ds(pl.multiple_of(column * BLOCK, BLOCK), BLOCK)] - 1).astype(jnp.float32)
    mean = turned * (1.0 / BLOCK) * my_signs
    bad = jnp.max(jnp.where(mean == mean, 0.0, 1.0), axis=(0, 1), keepdims=True)
    mean = jnp.where(bad > 0.0, jnp.nan, mean).astype(jnp.bfloat16)

    order = ("xyz", "yzx", "zxy")

    def moved(axis, delta):
        return (
            rem(x + delta, 4) if axis == "x" else x,
            rem(y + delta, 4) if axis == "y" else y,
            rem(z + delta, 4) if axis == "z" else z,
        )

    def at(p, core, where):
        a = {"x": where[0], "y": where[1], "z": where[2]}
        return (p, core, a[order[p][2]], a[order[p][1]], a[order[p][0]])

    def to_mate(p, phase, delta, ref, n):
        return remote(ref, ref, a_s.at[p, phase], a_r.at[p, n], dev(*moved(order[p][phase], delta), c))

    def small(p, phase, delta):
        return to_mate(p, phase, delta, gat.at[at(p, c, (x, y, z))[: 5 - phase]], phase)

    def mine(p, n):
        return {"x": x, "y": y, "z": z}[order[p][n]]

    def half_slab(p, ring, h):
        return gat.at[p, c, rem(mine(p, 2) + ring, 4), pl.ds(2 * h, 2)]

    def last(p, way, h, ring, n):
        return to_mate(p, 2, way, half_slab(p, ring, h), n)

    def forward(p, ring):
        ref = gat.at[p, c, rem(mine(p, 2) + ring, 4)]
        return remote(ref, ref, a_s.at[p, 3], f_r.at[p], sibling)

    for p in range(3):
        gat[at(p, c, (x, y, z))] = mean[p * PART : (p + 1) * PART]
        for delta in (1, 3, 2):
            small(p, 0, delta).start()
    for p in range(3):
        took(a_r.at[p, 0], 3 * PART)
        for delta in (1, 3, 2):
            small(p, 1, delta).start()

    def send_rotated(s, _):
        copy, here, t = r_copy(s)

        @pl.when(here)
        def _():
            rgot[pl.ds(pl.multiple_of(rem(t, 9) * SHARE, SHARE), SHARE), :] = rbuf[
                pl.ds(pl.multiple_of(s * SHARE, SHARE), SHARE), :
            ]

        @pl.when(jnp.logical_not(here))
        def _():
            copy.start()

        return 0

    lax.fori_loop(0, STAGES, send_rotated, 0)

    for ref, sem in (
        (out_, sib_s.at[0]), (sm, sib_s.at[1]),
        (z1.at[0:3, :, 0], z1_s.at[0]), (z1m.at[0:3], z1_s.at[1]), (z1.at[0:6], z1_s.at[2]), (z1m.at[0:6], z1_s.at[3]),
        (z2.at[0:3, :, 0], z2_s.at[0]), (z2m.at[0:3], z2_s.at[1]), (z2.at[0:6], z2_s.at[2]), (z2m.at[0:6], z2_s.at[3]),
        (xs.at[0:6, 0], x_s.at[0]), (xsm.at[0:6, 0], x_s.at[1]), (xs.at[0:3], x_s.at[2]), (xsm.at[0:3], x_s.at[3]),
        (gbuf.at[0:7], g_s),
    ):
        pltpu.make_async_copy(ref, ref, sem).wait()
    for p in range(3):
        took(a_r.at[p, 1], 12 * PART)
        last(p, 1, 0, 0, 2).start()
        last(p, 3, 1, 0, 3).start()
        last(p, 1, 1, 0, 4).start()
        last(p, 3, 0, 0, 4).start()
    for p in range(3):
        forward(p, 0).start()
    for p in range(3):
        took(a_r.at[p, 2], 8 * PART)
        last(p, 1, 0, 3, 5).start()
        took(a_r.at[p, 3], 8 * PART)
        last(p, 3, 1, 1, 5).start()
    for p in range(3):
        took(a_r.at[p, 4], 16 * PART)
        forward(p, 3).start()
        forward(p, 1).start()

    def drain_rotated(u, _):
        t = 9 * k + u

        @pl.when(jnp.logical_or(to_self == 0, rem(t, 4) != rem(g, 4)))
        def _():
            ref = rgot.at[pl.ds(pl.multiple_of(u * SHARE, SHARE), SHARE), :]
            remote(ref, ref, r_s.at[u], r_r.at[u], sibling).wait_recv()

        copy, here, _ = r_copy(u)

        @pl.when(jnp.logical_not(here))
        def _():
            copy.wait_send()

        return 0

    lax.fori_loop(0, STAGES, drain_rotated, 0)
    rot_ref[...] = rgot[...]
    for p in range(3):
        took(a_r.at[p, 5], 16 * PART)
        forward(p, 2).start()
    for p in range(3):
        took(f_r.at[p], 64 * PART)
    for p in range(3):
        for n, rows in enumerate((3, 12, 48, 64)):
            took(a_s.at[p, n], rows * PART)
    marks = jnp.zeros((16, BLOCK), jnp.float32)
    for core in range(2):
        for i in range(4):
            for j in range(4):
                for n in range(4):
                    marks = marks + gat[0, core, i, j, n, 0:16, :].astype(jnp.float32)
    bad_ref[0, 0] = jnp.max(jnp.where(marks == marks, 0.0, 1.0))


def fast(x_act, cotangent, sign_bits):
    bf16, f32, i16 = jnp.bfloat16, jnp.float32, jnp.int16
    dma = pltpu.SemaphoreType.DMA
    vmem = pltpu.VMEM
    return pl.pallas_call(
        kernel,
        out_shape=(
            jax.ShapeDtypeStruct((OWN, BLOCK), bf16),
            vmem((3, 2, 4, 4, 4, PART, BLOCK), bf16),
            jax.ShapeDtypeStruct((1, 1), f32),
        ),
        in_specs=[pl.BlockSpec(memory_space=pl.ANY)] + [pl.BlockSpec(memory_space=vmem)] * 2,
        out_specs=(
            pl.BlockSpec(memory_space=vmem),
            pl.BlockSpec(memory_space=vmem),
            pl.BlockSpec(memory_space=pltpu.SMEM),
        ),
        scratch_shapes=[
            vmem((TOK, D), bf16),
            vmem((KVW, KVW), bf16),
            vmem((512, 256), f32), vmem((512, 256), f32), vmem((512, 256), f32), vmem((512, 256), f32),
            vmem((STAGES, 2, 4, 256, BLOCK), bf16),
            vmem((STAGES, 2, 4, 256, BLOCK), bf16),
            vmem((STAGES, 2, 4, 256, BLOCK), bf16),
            vmem((STAGES, 2, 8, BLOCK), f32),
            vmem((STAGES, 2, 8, BLOCK), f32),
            vmem((STAGES, 2, 8, BLOCK), f32),
            vmem((2, 5, 8, BLOCK), f32),
            vmem((STAGES, 4, 256, BLOCK), f32),
            vmem((STAGES, 4, 8, BLOCK), f32),
            vmem((STAGES, 2, 2, 2, BLOCK, BLOCK), i16),
            vmem((STAGES, 2, 8, BLOCK), f32),
            vmem((STAGES, 2, 2, 2, BLOCK, BLOCK), i16),
            vmem((STAGES, 2, 8, BLOCK), f32),
            vmem((STAGES, 2, 2, BLOCK, BLOCK), i16),
            vmem((STAGES, 2, 8, BLOCK), f32),
            vmem((STAGES, 2, 2, BLOCK, BLOCK), i16),
            vmem((STAGES, 2, 8, BLOCK), f32),
            vmem((STAGES, 4, 256, BLOCK), i16),
            vmem((STAGES, 4, 8, BLOCK), f32),
            vmem((STAGES, 4, 256, BLOCK), i16),
            vmem((STAGES, 4, 8, BLOCK), f32),
            vmem((8, OWN, BLOCK), bf16),
            vmem((8, OWN, BLOCK), bf16),
            vmem((OWN, BLOCK), bf16),
            vmem((OWN, BLOCK), bf16),
            vmem((64 * PART, BLOCK), bf16),
            dma((2,)), dma((STAGES,)),
            dma((4,)), dma((STAGES, 2)),
            dma((4,)), dma((STAGES, 2)),
            dma((4,)), dma((STAGES,)),
            dma, dma((3,)),
            dma((STAGES,)), dma((STAGES,)),
            dma((3, 4)), dma((3, 6)),
            dma((3,)), dma,
        ],
        compiler_params=pltpu.CompilerParams(
            collective_id=0, has_side_effects=True, vmem_limit_bytes=47 * 2**20
        ),
        cost_estimate=pl.CostEstimate(flops=10**10, bytes_accessed=3 * 10**7, transcendentals=0),
        name="sync",
    )(x_act, cotangent, sign_bits.reshape(1, KVW))


def assemble_kernel(gat, rot_ref, rot_out, out_hbm, rows, sems):
    rot_out[...] = rot_ref[...]
    copies = []
    for quad in range(4):
        for s in range(STAGES):
            n = quad * STAGES + s
            for k in range(4):
                for g in range(8):
                    xh, z, c = quad // 2, (quad % 2) * 2 + k // 2, k % 2
                    x, y = xh * 2 + g // 4, g % 4
                    p, r = s // 3, (s % 3) * SHARE
                    where = ((z, y, x), (x, z, y), (y, x, z))[p]
                    column = 2 * k + g // 4
                    rows[
                        n, y * SHARE : (y + 1) * SHARE, column * BLOCK : (column + 1) * BLOCK
                    ] = gat[(p, c) + where + (slice(r, r + SHARE),)]
            copies.append(
                pltpu.make_async_copy(rows.at[n], out_hbm.at[pl.ds(n * BLOCK, BLOCK), :], sems.at[n])
            )
            copies[-1].start()
    for copy in copies:
        copy.wait()


def assemble(gathered, rotated):
    vmem = pl.BlockSpec(memory_space=pltpu.VMEM)
    return pl.pallas_call(
        assemble_kernel,
        out_shape=(
            jax.ShapeDtypeStruct((OWN, BLOCK), jnp.bfloat16),
            jax.ShapeDtypeStruct((D, KVW), jnp.bfloat16),
        ),
        in_specs=[vmem, vmem],
        out_specs=(vmem, pl.BlockSpec(memory_space=pl.ANY)),
        scratch_shapes=[
            pltpu.VMEM((4 * STAGES, BLOCK, KVW), jnp.bfloat16),
            pltpu.SemaphoreType.DMA((4 * STAGES,)),
        ],
        compiler_params=pltpu.CompilerParams(vmem_limit_bytes=24 * 2**20),
        cost_estimate=pl.CostEstimate(flops=0, bytes_accessed=2 * 10**7, transcendentals=0),
        name="assemble",
    )(gathered, rotated)


def hadamard():
    index_vals = jnp.arange(BLOCK)
    both = jnp.bitwise_and(index_vals[:, None], index_vals[None, :])
    parity = jnp.zeros_like(both)
    for bit_pos in range(7):
        parity = parity + jnp.bitwise_and(jnp.right_shift(both, bit_pos), 1)
    return (1 - 2 * (parity % 2)).astype(jnp.float32)


def rotate(matrix, signs, hmat):
    rows = matrix.shape[0]
    blocks = (matrix * signs[None, :]).reshape(rows, -1, BLOCK)
    turned = jnp.einsum("rbi,ij->rbj", blocks, hmat, precision=lax.Precision.HIGHEST)
    return turned.reshape(rows, -1)


def unrotate(matrix, signs, hmat):
    rows = matrix.shape[0]
    blocks = matrix.reshape(rows, -1, BLOCK)
    turned = jnp.einsum("rbi,ij->rbj", blocks, hmat, precision=lax.Precision.HIGHEST)
    return (turned / BLOCK).reshape(rows, -1) * signs[None, :]


def quantize(matrix):
    shape = matrix.shape
    blocks = matrix.reshape(shape[:-1] + (shape[-1] // BLOCK, BLOCK))
    largest = jnp.max(jnp.abs(blocks), axis=-1)
    powers = jnp.asarray([2.0**k for k in range(-7, 31)], dtype=jnp.float32)
    exceeds = largest[..., None] > 63.5 * powers
    scales = jnp.max(jnp.where(exceeds, powers, 0.00390625), axis=-1).astype(jnp.bfloat16)
    ratio = blocks / scales.astype(jnp.float32)[..., None]
    floored = jnp.floor(ratio)
    fraction = ratio - floored
    odd_level = floored - 2.0 * jnp.floor(0.5 * floored) == 1.0
    round_up = (fraction > 0.5) | (fraction == 0.5) & odd_level
    levels = (floored + round_up.astype(jnp.float32)).astype(jnp.bfloat16)
    return (levels.reshape(shape), scales)


def dequant(levels, scales):
    shape = levels.shape
    blocks = levels.astype(jnp.float32).reshape(shape[:-1] + (shape[-1] // BLOCK, BLOCK))
    return (blocks * scales.astype(jnp.float32)[..., None]).reshape(shape)


def general(x_act, cotangent, sign_bits):
    signs = (2 * sign_bits - 1).astype(jnp.float32)
    hmat = hadamard()
    local = lax.dot_general(
        x_act, cotangent, (((0,), (0,)), ((), ())), preferred_element_type=jnp.float32
    )
    levels, scales = quantize(rotate(local, signs, hmat))
    width = levels.shape[1]
    members = lax.axis_size("dev")
    groups = lax.axis_size("group")
    rows = levels.shape[0] // members
    got_levels, got_scales = (
        lax.all_to_all(
            levels.reshape(members, rows, width), "dev", split_axis=0, concat_axis=0, tiled=True
        ),
        lax.all_to_all(
            scales.reshape(members, rows, width // BLOCK),
            "dev",
            split_axis=0,
            concat_axis=0,
            tiled=True,
        ),
    )
    group_total = jnp.sum(dequant(got_levels, got_scales), axis=0)
    part = dequant(*quantize(group_total)).astype(jnp.bfloat16)
    blocks = part.reshape(rows, groups, BLOCK).swapaxes(0, 1)
    arrived = lax.all_to_all(blocks, "group", split_axis=0, concat_axis=0, tiled=True).astype(jnp.float32)
    running = arrived[0]
    for other in range(1, groups):
        running = dequant(*quantize(running + arrived[other]))
    total = running / (groups * members)
    position = lax.axis_index("group")
    my_signs = lax.dynamic_slice_in_dim(signs, position * BLOCK, BLOCK, 0)
    mean = unrotate(total, my_signs, hmat).astype(jnp.bfloat16)
    every = jnp.broadcast_to(mean[None], (groups, rows, BLOCK))
    every = lax.all_to_all(every, "group", split_axis=0, concat_axis=0, tiled=True)
    every = jnp.broadcast_to(every[None], (members, groups, rows, BLOCK))
    every = lax.all_to_all(every, "dev", split_axis=0, concat_axis=0, tiled=True)
    every = every.swapaxes(1, 2).reshape(members * rows, width)
    return (total.astype(jnp.bfloat16), every)


def body(x_act, cotangent, sign_bits):
    rotated, gathered, inexact = fast(x_act, cotangent, sign_bits)
    rotated, mean = assemble(gathered, rotated)
    _, rotated, mean = lax.while_loop(
        lambda state: state[0] > 0.0,
        lambda state: (jnp.float32(0.0), *general(x_act, cotangent, sign_bits)),
        (inexact[0, 0], rotated, mean),
    )
    return rotated, mean


def solution(mesh):
    placed = (P(("group", "dev"), None), P(("group", "dev"), None), P())
    return jax.shard_map(
        body, mesh=mesh, in_specs=placed, out_specs=(P("dev", "group"), P()), check_vma=False
    )
```

```python
import functools

import jax
import jax.numpy as jnp
from jax import lax
from jax.experimental import pallas as pl
from jax.experimental.pallas import tpu as pltpu
from jax.sharding import PartitionSpec as P

BLOCK = 128
TOK = 320
D = 4608
KVW = 1024
STAGES = 9
QUAD = 1152
OWN = 288
PART = 96
SHARE = 32
LAG_A, LAG_B, LAG_C, LAG_D = 1, 5, 8, 10
MAGIC = 12582912.0
MESH = pl.DeviceIdType.MESH
GATHERS = (("xyz", 0, 64), ("yzx", 64, 64), ("zxy", 128, 64), ("xyz", 192, 32), ("yzx", 224, 32), ("zxy", 256, 32))


def hadamard_in_kernel():
    i = lax.broadcasted_iota(jnp.int32, (BLOCK, BLOCK), 0)
    j = lax.broadcasted_iota(jnp.int32, (BLOCK, BLOCK), 1)
    both = i & j
    parity = jnp.zeros_like(both)
    for bit in range(7):
        parity = parity + ((both >> bit) & 1)
    return (1 - 2 * (parity & 1)).astype(jnp.float32).astype(jnp.bfloat16)


def scale_of(largest):
    scale = jnp.full_like(largest, 2.0**-8)
    for e in (32, 16, 8, 4, 2, 1):
        cand = scale * 2.0**e
        scale = jnp.where(largest > cand * 63.5, cand, scale)
    return jnp.minimum(scale, 2.0**30)


def rounded(value, scale):
    shift = scale * MAGIC
    return (value + shift) - shift


def inverse_of(power):
    scale = jnp.full_like(power, 2.0**-8)
    inv = jnp.full_like(power, 2.0**8)
    for e in (32, 16, 8, 4, 2, 1):
        cand = scale * 2.0**e
        take = power >= cand
        scale = jnp.where(take, cand, scale)
        inv = jnp.where(take, inv * 2.0**-e, inv)
    return inv


def on_wire(unit, total):
    inv = inverse_of(unit)
    exact = total * inv * 127.0 <= 32767.0
    return inv, jnp.where(exact, unit, jnp.nan), jnp.where(exact, total, jnp.nan)


def kernel(
    x_hbm, cot_hbm, sb_ref, rot_ref, early, late, bad_ref,
    xv, ct3, tmp0, tmp1, tmp2, tmp3, own, out_, got, om, sm, gm, pw, acc, accm,
    z1, z1m, z1r, z1rm, z2, z2m, z2r, z2rm, xs, xsm, xr, xrm, gbuf, parts, rbuf, rgot, gauge, cot_ref,
    sib_s, sib_r, z1_s, z1_r, z2_s, z2_r, x_s, x_r, g_s, g_r, r_s, r_r, a_s, a_r, f_r, l_s,
):
    g = lax.axis_index("group")
    d = lax.axis_index("dev")
    div, rem = (lambda a, b: lax.div(a, jnp.int32(b))), (lambda a, b: lax.rem(a, jnp.int32(b)))
    xl, y = div(g, 4), rem(g, 4)
    xh, z, c = div(d, 8), rem(div(d, 2), 4), rem(d, 2)
    z_hi, k = div(z, 2), rem(z, 2) * 2 + c
    x = xh * 2 + xl

    def dev(xx, yy, zz, cc):
        return (rem(xx, 2) * 4 + yy, div(xx, 2) * 8 + zz * 2 + cc)

    sibling = dev(x, y, z, 1 - c)
    partner = dev((x + 2) % 4, y, z, c)
    beside = (dev(x, y, (z + 1) % 4, c), dev(x, y, (z + 3) % 4, c))
    column = 2 * k + g // 4
    to_self = jnp.logical_and(k == g // 2, g % 2 == g // 4).astype(jnp.int32)

    fetch_cot = pltpu.make_async_copy(cot_hbm, cot_ref, l_s.at[0])
    fetch_cot.start()
    fetch = pltpu.make_async_copy(x_hbm, xv, l_s.at[1])
    fetch.start()

    bar = pltpu.get_barrier_semaphore()

    def greet(who):
        pl.semaphore_signal(bar, inc=1, device_id=who, device_id_type=MESH)

    greet(sibling)
    for delta in (1, 2, 3):
        greet(dev((x + delta) % 4, y, z, c))
        greet(dev(x, (y + delta) % 4, z, c))
        greet(dev(x, y, (z + delta) % 4, c))
    for delta in (1, 2, 3):
        greet(dev(xh * 2 + 1 - xl, (y + delta) % 4, z, c))
    ksrc = g // 2
    for m in range(4):

        @pl.when(jnp.logical_or(to_self == 0, m != g % 4))
        def _():
            greet(((g % 2) * 4 + m, xh * 8 + (z_hi * 2 + ksrc // 2) * 2 + ksrc % 2))

    hmat = hadamard_in_kernel()
    signs = (2 * sb_ref[...] - 1).astype(jnp.float32)
    fetch_cot.wait()
    for blk in range(8):
        cols = slice(blk * BLOCK, (blk + 1) * BLOCK)
        signed = (cot_ref[:, cols].astype(jnp.float32) * signs[:, cols]).astype(jnp.bfloat16)
        turned = lax.dot_general(hmat, signed, (((1,), (1,)), ((), ())), preferred_element_type=jnp.float32)
        hi = turned.astype(jnp.bfloat16)
        rest = turned - hi.astype(jnp.float32)
        mid = rest.astype(jnp.bfloat16)
        low = (rest - mid.astype(jnp.float32)).astype(jnp.bfloat16)
        kk, b = blk // 2, blk % 2
        r0 = (kk % 2) * 512 + (kk // 2) * 256 + b * BLOCK
        rows = slice(r0, r0 + BLOCK)
        for n, term in enumerate((hi, mid, low)):
            ct3[rows, n * 256 : (n + 1) * 256] = term[:, :256]
        ct3[rows, 768:896] = jnp.concatenate([hi[:, 256:], mid[:, 256:]], axis=1)
        ct3[rows, 896:1024] = jnp.concatenate([low[:, 256:], jnp.zeros((BLOCK, 64), jnp.bfloat16)], axis=1)

    def product(s, core, X, tmp):
        lanes = [pl.ds(pl.multiple_of(X * 2304 + h * QUAD + s * BLOCK, BLOCK), BLOCK) for h in (0, 1)]
        xa = jnp.concatenate([xv[:, l] for l in lanes], axis=1)
        x3 = jnp.concatenate([xa[:256]] * 3 + [xa[256:]] * 3 + [jnp.zeros((64, 256), jnp.bfloat16)], axis=0)
        lhs = ct3[pl.ds(pl.multiple_of(core * 512, 512), 512), :]
        tmp[...] = jnp.dot(lhs, x3, preferred_element_type=jnp.float32)

    def quantized(s, X, tmp, lev, met):
        def sub(Z, b):
            r0, l0 = (Z % 2) * 256 + b * BLOCK, (Z // 2) * BLOCK
            return tmp[r0 : r0 + BLOCK, l0 : l0 + BLOCK]

        largest = jnp.concatenate(
            [jnp.max(jnp.abs(sub(Z, b)), axis=0, keepdims=True) for Z in range(4) for b in range(2)], axis=0
        )
        scale = scale_of(largest)
        met[s, X] = scale
        for Z in range(4):
            for b in range(2):
                r = Z * 2 + b
                lev[s, X, Z, half(b), :] = rounded(sub(Z, b), scale[r : r + 1]).astype(jnp.bfloat16)

    def half(b):
        return slice(b * BLOCK, (b + 1) * BLOCK)

    def remote(src, dst, ss, rs, who):
        return pltpu.make_async_remote_copy(src, dst, ss, rs, device_id=who, device_id_type=MESH)

    def both(src, srcm, dst, dstm, ss, n, rs, who):
        return (remote(src, dst, ss.at[2 * n], rs, who), remote(srcm, dstm, ss.at[2 * n + 1], rs, who))

    def sib_copies(s):
        return both(out_.at[s], sm.at[s], got.at[s], gm.at[s], sib_s, 0, sib_r.at[s], sibling)

    def z1_copies(s, way, n):
        a, b = z1.at[s, way], z1r.at[s, way]
        if n == 1:
            a, b = a.at[0], b.at[0]
        return both(a, z1m.at[s, way], b, z1rm.at[s, way], z1_s, n - 1, z1_r.at[s, way], beside[way])

    def z2_copies(s, way, n):
        a, b = z2.at[s, way], z2r.at[s, way]
        if n == 1:
            a, b = a.at[0], b.at[0]
        return both(a, z2m.at[s, way], b, z2rm.at[s, way], z2_s, n - 1, z2_r.at[s, way], beside[way])

    def x_copies(s, n):
        a, am, b, bm = xs.at[s], xsm.at[s], xr.at[s], xrm.at[s]
        if n == 1:
            a, am, b, bm = a.at[0], am.at[0], b.at[0], bm.at[0]
        return both(a, am, b, bm, x_s, 0 if n == 1 else 1, x_r.at[s], partner)

    def took(sem, rows):
        ref = gauge.at[pl.ds(0, rows), :]
        pltpu.make_async_copy(ref, ref, sem).wait()

    def g_copy(p, q):
        to = rem(g + q, 8)
        three = pl.ds(pl.multiple_of(p * PART, PART), PART)
        return remote(gbuf.at[to, three, :], parts.at[g, three, :], g_s, g_r.at[p], (to, d))

    def r_copy(s):
        t = 4 * s + rem(g, 4)
        j = div(t, 9)
        src = rbuf.at[pl.ds(pl.multiple_of(s * SHARE, SHARE), SHARE), :]
        dst = rgot.at[pl.ds(pl.multiple_of(rem(t, 9) * SHARE, SHARE), SHARE), :]
        who = (column, xh * 8 + (z_hi * 2 + div(j, 2)) * 2 + rem(j, 2))
        return remote(src, dst, r_s.at[s], r_r.at[rem(t, 9)], who), jnp.logical_and(to_self == 1, j == k), t

    def start(copies):
        for copy in copies:
            copy.start()

    def encode(value, inv):
        return (value * inv).astype(jnp.int16)

    def pair_block(s, X, Z, b):
        return own[s, X, Z, half(b), :].astype(jnp.float32) + got[s, X, Z, half(b), :].astype(jnp.float32)

    def add(s, i, b, block, unit, total):
        acc[s, i, half(b), :] = acc[s, i, half(b), :] + block.astype(jnp.float32) * unit
        accm[s, i, b : b + 1, :] = jnp.minimum(accm[s, i, b : b + 1, :], unit)
        accm[s, i, 2 + b : 3 + b, :] = accm[s, i, 2 + b : 3 + b, :] + total

    def packed(s, i, b):
        inv, unit, total = on_wire(accm[s, i, b : b + 1, :], accm[s, i, 2 + b : 3 + b, :])
        return encode(acc[s, i, half(b), :], inv), unit, total

    def z1_from_sums(s):
        two = (z + 2) % 4
        for way, (near, b) in enumerate((((z + 1) % 4, 1), ((z + 3) % 4, 0))):
            for kind, (i, bb) in enumerate(((near, b), (two, 1 - b))):
                block, unit, total = packed(s, i, bb)
                z1[s, way, 0, kind] = block
                z1m[s, way, kind : kind + 1, :] = unit
                z1m[s, way, 2 + kind : 3 + kind, :] = total
            start(z1_copies(s, way, 1))

    def z1_take(s, n, mine, right, left_):
        for way in (0, 1):
            took(z1_r.at[s, way], 256 * n + 16)
            for i in range(n):
                r = 4 * i
                b = way
                on = right(i) if way == 0 else left_(i)
                add(s, on, b, z1r[s, way, i, 1], z1rm[s, way, r + 1 : r + 2, :], z1rm[s, way, r + 3 : r + 4, :])
                block, unit, total = packed(s, on, b)
                z2[s, way, i] = block
                z2m[s, way, i : i + 1, :] = unit
                z2m[s, way, 2 + i : 3 + i, :] = total
            start(z2_copies(s, way, n))
            for i in range(n):
                r = 4 * i
                add(s, mine(i), 1 - way, z1r[s, way, i, 0], z1rm[s, way, r : r + 1, :], z1rm[s, way, r + 2 : r + 3, :])

    def z2_take(s, n, mine):
        for way in (0, 1):
            took(z2_r.at[s, way], 128 * n + 16)
            for i in range(n):
                add(s, mine(i), way, z2r[s, way, i], z2rm[s, way, i : i + 1, :], z2rm[s, way, 2 + i : 3 + i, :])

    def along_z_first(s):
        return rem(s, 3) != 1

    def step_a(s):
        took(sib_r.at[s], 2080)
        for X in (0, 1):
            unit = jnp.minimum(om[s, X], gm[s, X])
            total = om[s, X] + gm[s, X]
            inv, wire_unit, wire_total = on_wire(unit, total)
            for n, v in enumerate((unit, total, inv, wire_unit, wire_total)):
                pw[X, n] = v

        def row(X, n, Z, b):
            return pw[X, n, pl.ds(2 * Z + b, 1), :]

        def keep(i, ii, X, Z, b):
            acc[s, i, half(ii), :] = pair_block(s, X, Z, b)
            accm[s, i, ii : ii + 1, :] = row(X, 0, Z, b)
            accm[s, i, 2 + ii : 3 + ii, :] = row(X, 1, Z, b)

        @pl.when(along_z_first(s))
        def _():
            two, after, before = (z + 2) % 4, (z + 1) % 4, (z + 3) % 4
            for way, (near, b) in enumerate(((after, 1), (before, 0))):
                for X in (0, 1):
                    for kind, (Z, bb) in enumerate(((near, b), (two, 1 - b))):
                        z1[s, way, X, kind] = encode(pair_block(s, X, Z, bb), row(X, 2, Z, bb))
                        z1m[s, way, 4 * X + kind : 4 * X + kind + 1, :] = row(X, 3, Z, bb)
                        z1m[s, way, 4 * X + 2 + kind : 4 * X + 3 + kind, :] = row(X, 4, Z, bb)
                start(z1_copies(s, way, 2))
            for X in (0, 1):
                for b in (0, 1):
                    keep(X, b, X, z, b)
                keep(2 + X, 0, X, after, 0)
                keep(2 + X, 1, X, before, 1)

        @pl.when(jnp.logical_not(along_z_first(s)))
        def _():
            for Z in range(4):
                for b in (0, 1):
                    xs[s, Z, half(b), :] = encode(pair_block(s, 1 - xh, Z, b), row(1 - xh, 2, Z, b))
                    xsm[s, Z, b : b + 1, :] = row(1 - xh, 3, Z, b)
                    xsm[s, Z, 2 + b : 3 + b, :] = row(1 - xh, 4, Z, b)
            start(x_copies(s, 4))
            for Z in range(4):
                for b in (0, 1):
                    keep(Z, b, xh, Z, b)

    def x_take(s, i, n):
        for b in (0, 1):
            add(s, i, b, xr[s, n, half(b), :], xrm[s, n, b : b + 1, :], xrm[s, n, 2 + b : 3 + b, :])

    def step_b(s):
        @pl.when(along_z_first(s))
        def _():
            z1_take(s, 2, lambda i: i, lambda i: 2 + i, lambda i: 2 + i)

        @pl.when(jnp.logical_not(along_z_first(s)))
        def _():
            took(x_r.at[s], 1088)
            for Z in range(4):
                x_take(s, Z, Z)
            z1_from_sums(s)

    def step_c(s):
        @pl.when(along_z_first(s))
        def _():
            z2_take(s, 2, lambda i: i)
            for b in (0, 1):
                block, unit, total = packed(s, 1 - xh, b)
                xs[s, 0, half(b), :] = block
                xsm[s, 0, b : b + 1, :] = unit
                xsm[s, 0, 2 + b : 3 + b, :] = total
            start(x_copies(s, 1))

        @pl.when(jnp.logical_not(along_z_first(s)))
        def _():
            z1_take(s, 1, lambda i: z, lambda i: (z + 1) % 4, lambda i: (z + 3) % 4)

    def step_d(s):
        @pl.when(along_z_first(s))
        def _():
            took(x_r.at[s], 272)
            x_take(s, xh, 0)

        @pl.when(jnp.logical_not(along_z_first(s)))
        def _():
            z2_take(s, 1, lambda i: z)

        i = jnp.where(along_z_first(s), xh, z)
        sums = [acc[s, i, half(b), :] for b in (0, 1)]
        largest = jnp.concatenate([jnp.max(jnp.abs(t), axis=0, keepdims=True) for t in sums], axis=0)
        scale = scale_of(largest)
        for b in (0, 1):
            value = rounded(sums[b], scale[b : b + 1])
            value = value.T.astype(jnp.bfloat16)
            for m in range(4):
                gbuf[4 * b + m, pl.ds(pl.multiple_of(s * SHARE, SHARE), SHARE), :] = value[m * SHARE : (m + 1) * SHARE]

        @pl.when(rem(s, 3) == 2)
        def _():
            for q in range(1, 8):
                g_copy(div(s, 3), q).start()

    def moved(axis, delta):
        return (
            rem(x + delta, 4) if axis == "x" else x,
            rem(y + delta, 4) if axis == "y" else y,
            rem(z + delta, 4) if axis == "z" else z,
        )

    def mine(j, n):
        return {"x": x, "y": y, "z": z}[GATHERS[j][0][n]]

    def held(j, core, *index):
        ref, n = (early, j) if j < 3 else (late, j - 3)
        return ref.at[(n, core) + index]

    def to_mate(j, phase, delta, ref, n):
        who = dev(*moved(GATHERS[j][0][phase], delta), c)
        return remote(ref, ref, a_s.at[j, phase], a_r.at[j, n], who)

    def half_slab(j, ring, h):
        return held(j, c, rem(mine(j, 2) + ring, 4), pl.ds(2 * h, 2))

    def last(j, way, h, ring, n):
        to_mate(j, 2, way, half_slab(j, ring, h), n).start()

    def forward(j, ring):
        ref = held(j, c, rem(mine(j, 2) + ring, 4))
        remote(ref, ref, a_s.at[j, 3], f_r.at[j], sibling).start()

    def phase0(j, mean):
        block = held(j, c, mine(j, 2), mine(j, 1), mine(j, 0))
        block[...] = mean
        for delta in (1, 3, 2):
            to_mate(j, 0, delta, block, 0).start()

    def phase1(j):
        took(a_r.at[j, 0], 3 * GATHERS[j][2])
        for delta in (1, 3, 2):
            to_mate(j, 1, delta, held(j, c, mine(j, 2), mine(j, 1)), 1).start()

    def phase2(j):
        took(a_r.at[j, 1], 12 * GATHERS[j][2])
        last(j, 1, 0, 0, 2)
        last(j, 3, 1, 0, 3)
        last(j, 1, 1, 0, 4)
        last(j, 3, 0, 0, 4)
        forward(j, 0)

    def relay(j):
        took(a_r.at[j, 2], 8 * GATHERS[j][2])
        last(j, 1, 0, 3, 5)
        took(a_r.at[j, 3], 8 * GATHERS[j][2])
        last(j, 3, 1, 1, 5)

    def spread(j):
        took(a_r.at[j, 4], 16 * GATHERS[j][2])
        forward(j, 3)
        forward(j, 1)

    def finish(j):
        took(a_r.at[j, 5], 16 * GATHERS[j][2])
        forward(j, 2)

    fetch.wait()

    def loop(t, _):
        @pl.when(t < STAGES)
        def _():
            product(t, 1 - c, 0, tmp0)
            product(t, 1 - c, 1, tmp1)
            quantized(t, 0, tmp0, out_, sm)
            product(t, c, 0, tmp2)
            quantized(t, 1, tmp1, out_, sm)
            product(t, c, 1, tmp3)

            @pl.when(t == 0)
            def _():
                pl.semaphore_wait(bar, 17 - to_self)

            start(sib_copies(t))
            quantized(t, 0, tmp2, own, om)
            quantized(t, 1, tmp3, own, om)

        for lag, step in ((LAG_A, step_a), (LAG_B, step_b), (LAG_C, step_c), (LAG_D, step_d)):

            @pl.when(jnp.logical_and(t >= lag, t < STAGES + lag))
            def _():
                step(t - lag)

        return 0

    lax.fori_loop(0, STAGES + LAG_D, loop, 0)

    parts[g] = gbuf[g]
    for p in range(3):
        took(g_r.at[p], 7 * PART)
    total = parts[0].astype(jnp.float32)
    for other in range(1, 8):
        total = total + parts[other].astype(jnp.float32)
        total = rounded(total, scale_of(jnp.max(jnp.abs(total), axis=1, keepdims=True)))
    total = total * (1.0 / 128.0)
    rbuf[...] = total.astype(jnp.bfloat16)
    turned = jnp.dot(total.astype(jnp.bfloat16), hmat, preferred_element_type=jnp.float32)
    my_signs = (2 * sb_ref[:, pl.ds(pl.multiple_of(column * BLOCK, BLOCK), BLOCK)] - 1).astype(jnp.float32)
    mean = turned * (1.0 / BLOCK) * my_signs
    bad = jnp.max(jnp.where(mean == mean, 0.0, 1.0), axis=(0, 1), keepdims=True)
    mean = jnp.where(bad > 0.0, jnp.nan, mean).astype(jnp.bfloat16)

    for j, (_, row, rows) in enumerate(GATHERS):
        phase0(j, mean[row : row + rows])
    for j in range(6):
        phase1(j)

    for j in range(6):
        phase2(j)

    def send_rotated(s, _):
        copy, here, t = r_copy(s)

        @pl.when(here)
        def _():
            rgot[pl.ds(pl.multiple_of(rem(t, 9) * SHARE, SHARE), SHARE), :] = rbuf[
                pl.ds(pl.multiple_of(s * SHARE, SHARE), SHARE), :
            ]

        @pl.when(jnp.logical_not(here))
        def _():
            copy.start()

        return 0

    lax.fori_loop(0, STAGES, send_rotated, 0)
    for ref, sem in (
        (out_, sib_s.at[0]), (sm, sib_s.at[1]),
        (z1.at[0:3, :, 0], z1_s.at[0]), (z1m.at[0:3], z1_s.at[1]), (z1.at[0:6], z1_s.at[2]), (z1m.at[0:6], z1_s.at[3]),
        (z2.at[0:3, :, 0], z2_s.at[0]), (z2m.at[0:3], z2_s.at[1]), (z2.at[0:6], z2_s.at[2]), (z2m.at[0:6], z2_s.at[3]),
        (xs.at[0:6, 0], x_s.at[0]), (xsm.at[0:6, 0], x_s.at[1]), (xs.at[0:3], x_s.at[2]), (xsm.at[0:3], x_s.at[3]),
        (gbuf.at[0:7], g_s),
    ):
        pltpu.make_async_copy(ref, ref, sem).wait()
    for j in range(3):
        relay(j)
    for j in range(3):
        spread(j)
    for j in range(3, 6):
        relay(j)
    for j in range(3, 6):
        spread(j)

    def drain_rotated(u, _):
        t = 9 * k + u

        @pl.when(jnp.logical_or(to_self == 0, rem(t, 4) != rem(g, 4)))
        def _():
            ref = rgot.at[pl.ds(pl.multiple_of(u * SHARE, SHARE), SHARE), :]
            remote(ref, ref, r_s.at[u], r_r.at[u], sibling).wait_recv()

        copy, here, _ = r_copy(u)

        @pl.when(jnp.logical_not(here))
        def _():
            copy.wait_send()

        return 0

    lax.fori_loop(0, STAGES, drain_rotated, 0)
    rot_ref[...] = rgot[...]
    for j in range(6):
        finish(j)
    for j in range(6):
        took(f_r.at[j], 64 * GATHERS[j][2])
    for j in range(6):
        for n, blocks in enumerate((3, 12, 48, 64)):
            took(a_s.at[j, n], blocks * GATHERS[j][2])
    marks = jnp.zeros((16, BLOCK), jnp.float32)
    for core in range(2):
        for i in range(4):
            for j in range(4):
                for n in range(4):
                    marks = marks + late[2, core, i, j, n, 0:16, :].astype(jnp.float32)
    bad_ref[0, 0] = jnp.max(jnp.where(marks == marks, 0.0, 1.0))


def fast(x_act, cotangent, sign_bits):
    bf16, f32, i16 = jnp.bfloat16, jnp.float32, jnp.int16
    dma = pltpu.SemaphoreType.DMA
    vmem = pltpu.VMEM
    return pl.pallas_call(
        kernel,
        out_shape=(
            vmem((OWN, BLOCK), bf16),
            vmem((3, 2, 4, 4, 4, 2 * SHARE, BLOCK), bf16),
            vmem((3, 2, 4, 4, 4, SHARE, BLOCK), bf16),
            jax.ShapeDtypeStruct((1, 1), f32),
        ),
        in_specs=[pl.BlockSpec(memory_space=pl.ANY)] * 2 + [pl.BlockSpec(memory_space=vmem)],
        out_specs=(
            pl.BlockSpec(memory_space=vmem),
            pl.BlockSpec(memory_space=vmem),
            pl.BlockSpec(memory_space=vmem),
            pl.BlockSpec(memory_space=pltpu.SMEM),
        ),
        scratch_shapes=[
            vmem((TOK, D), bf16),
            vmem((KVW, KVW), bf16),
            vmem((512, 256), f32), vmem((512, 256), f32), vmem((512, 256), f32), vmem((512, 256), f32),
            vmem((STAGES, 2, 4, 256, BLOCK), bf16),
            vmem((STAGES, 2, 4, 256, BLOCK), bf16),
            vmem((STAGES, 2, 4, 256, BLOCK), bf16),
            vmem((STAGES, 2, 8, BLOCK), f32),
            vmem((STAGES, 2, 8, BLOCK), f32),
            vmem((STAGES, 2, 8, BLOCK), f32),
            vmem((2, 5, 8, BLOCK), f32),
            vmem((STAGES, 4, 256, BLOCK), f32),
            vmem((STAGES, 4, 8, BLOCK), f32),
            vmem((STAGES, 2, 2, 2, BLOCK, BLOCK), i16),
            vmem((STAGES, 2, 8, BLOCK), f32),
            vmem((STAGES, 2, 2, 2, BLOCK, BLOCK), i16),
            vmem((STAGES, 2, 8, BLOCK), f32),
            vmem((STAGES, 2, 2, BLOCK, BLOCK), i16),
            vmem((STAGES, 2, 8, BLOCK), f32),
            vmem((STAGES, 2, 2, BLOCK, BLOCK), i16),
            vmem((STAGES, 2, 8, BLOCK), f32),
            vmem((STAGES, 4, 256, BLOCK), i16),
            vmem((STAGES, 4, 8, BLOCK), f32),
            vmem((STAGES, 4, 256, BLOCK), i16),
            vmem((STAGES, 4, 8, BLOCK), f32),
            vmem((8, OWN, BLOCK), bf16),
            vmem((8, OWN, BLOCK), bf16),
            vmem((OWN, BLOCK), bf16),
            vmem((OWN, BLOCK), bf16),
            vmem((64 * PART, BLOCK), bf16),
            vmem((TOK, KVW), bf16),
            dma((2,)), dma((STAGES,)),
            dma((4,)), dma((STAGES, 2)),
            dma((4,)), dma((STAGES, 2)),
            dma((4,)), dma((STAGES,)),
            dma, dma((3,)),
            dma((STAGES,)), dma((STAGES,)),
            dma((6, 4)), dma((6, 6)),
            dma((6,)), dma((2,)),
        ],
        compiler_params=pltpu.CompilerParams(
            collective_id=0, has_side_effects=True, vmem_limit_bytes=53 * 2**20
        ),
        cost_estimate=pl.CostEstimate(flops=10**10, bytes_accessed=3 * 10**7, transcendentals=0),
        name="sync",
    )(x_act, cotangent, sign_bits.reshape(1, KVW))


def assemble_kernel(early, late, rot_ref, rot_out, out_hbm, rows, sems):
    rot_out[...] = rot_ref[...]
    copies = []
    for quad in range(4):
        for s in range(STAGES):
            n = quad * STAGES + s
            for k in range(4):
                for g in range(8):
                    xh, z, c = quad // 2, (quad % 2) * 2 + k // 2, k % 2
                    x, y = xh * 2 + g // 4, g % 4
                    ref, j, r = (early, s // 2, s % 2 * SHARE) if s < 6 else (late, s - 6, 0)
                    axes = GATHERS[j if s < 6 else j + 3][0]
                    where = tuple({"x": x, "y": y, "z": z}[axes[n_axis]] for n_axis in (2, 1, 0))
                    column = 2 * k + g // 4
                    rows[
                        n, y * SHARE : (y + 1) * SHARE, column * BLOCK : (column + 1) * BLOCK
                    ] = ref[(j, c) + where + (slice(r, r + SHARE),)]
            copies.append(
                pltpu.make_async_copy(rows.at[n], out_hbm.at[pl.ds(n * BLOCK, BLOCK), :], sems.at[n])
            )
            copies[-1].start()
    for copy in copies:
        copy.wait()


def assemble(early, late, rotated):
    vmem = pl.BlockSpec(memory_space=pltpu.VMEM)
    return pl.pallas_call(
        assemble_kernel,
        out_shape=(
            jax.ShapeDtypeStruct((OWN, BLOCK), jnp.bfloat16),
            jax.ShapeDtypeStruct((D, KVW), jnp.bfloat16),
        ),
        in_specs=[vmem, vmem, vmem],
        out_specs=(vmem, pl.BlockSpec(memory_space=pl.ANY)),
        scratch_shapes=[
            pltpu.VMEM((4 * STAGES, BLOCK, KVW), jnp.bfloat16),
            pltpu.SemaphoreType.DMA((4 * STAGES,)),
        ],
        compiler_params=pltpu.CompilerParams(vmem_limit_bytes=24 * 2**20),
        cost_estimate=pl.CostEstimate(flops=0, bytes_accessed=2 * 10**7, transcendentals=0),
        name="assemble",
    )(early, late, rotated)


def hadamard():
    index_vals = jnp.arange(BLOCK)
    both = jnp.bitwise_and(index_vals[:, None], index_vals[None, :])
    parity = jnp.zeros_like(both)
    for bit_pos in range(7):
        parity = parity + jnp.bitwise_and(jnp.right_shift(both, bit_pos), 1)
    return (1 - 2 * (parity % 2)).astype(jnp.float32)


def rotate(matrix, signs, hmat):
    rows = matrix.shape[0]
    blocks = (matrix * signs[None, :]).reshape(rows, -1, BLOCK)
    turned = jnp.einsum("rbi,ij->rbj", blocks, hmat, precision=lax.Precision.HIGHEST)
    return turned.reshape(rows, -1)


def unrotate(matrix, signs, hmat):
    rows = matrix.shape[0]
    blocks = matrix.reshape(rows, -1, BLOCK)
    turned = jnp.einsum("rbi,ij->rbj", blocks, hmat, precision=lax.Precision.HIGHEST)
    return (turned / BLOCK).reshape(rows, -1) * signs[None, :]


def quantize(matrix):
    shape = matrix.shape
    blocks = matrix.reshape(shape[:-1] + (shape[-1] // BLOCK, BLOCK))
    largest = jnp.max(jnp.abs(blocks), axis=-1)
    powers = jnp.asarray([2.0**k for k in range(-7, 31)], dtype=jnp.float32)
    exceeds = largest[..., None] > 63.5 * powers
    scales = jnp.max(jnp.where(exceeds, powers, 0.00390625), axis=-1).astype(jnp.bfloat16)
    ratio = blocks / scales.astype(jnp.float32)[..., None]
    floored = jnp.floor(ratio)
    fraction = ratio - floored
    odd_level = floored - 2.0 * jnp.floor(0.5 * floored) == 1.0
    round_up = (fraction > 0.5) | (fraction == 0.5) & odd_level
    levels = (floored + round_up.astype(jnp.float32)).astype(jnp.bfloat16)
    return (levels.reshape(shape), scales)


def dequant(levels, scales):
    shape = levels.shape
    blocks = levels.astype(jnp.float32).reshape(shape[:-1] + (shape[-1] // BLOCK, BLOCK))
    return (blocks * scales.astype(jnp.float32)[..., None]).reshape(shape)


def general(x_act, cotangent, sign_bits):
    signs = (2 * sign_bits - 1).astype(jnp.float32)
    hmat = hadamard()
    local = lax.dot_general(
        x_act, cotangent, (((0,), (0,)), ((), ())), preferred_element_type=jnp.float32
    )
    levels, scales = quantize(rotate(local, signs, hmat))
    width = levels.shape[1]
    members = lax.axis_size("dev")
    groups = lax.axis_size("group")
    rows = levels.shape[0] // members
    got_levels, got_scales = (
        lax.all_to_all(
            levels.reshape(members, rows, width), "dev", split_axis=0, concat_axis=0, tiled=True
        ),
        lax.all_to_all(
            scales.reshape(members, rows, width // BLOCK),
            "dev",
            split_axis=0,
            concat_axis=0,
            tiled=True,
        ),
    )
    group_total = jnp.sum(dequant(got_levels, got_scales), axis=0)
    part = dequant(*quantize(group_total)).astype(jnp.bfloat16)
    blocks = part.reshape(rows, groups, BLOCK).swapaxes(0, 1)
    arrived = lax.all_to_all(blocks, "group", split_axis=0, concat_axis=0, tiled=True).astype(jnp.float32)
    running = arrived[0]
    for other in range(1, groups):
        running = dequant(*quantize(running + arrived[other]))
    total = running / (groups * members)
    position = lax.axis_index("group")
    my_signs = lax.dynamic_slice_in_dim(signs, position * BLOCK, BLOCK, 0)
    mean = unrotate(total, my_signs, hmat).astype(jnp.bfloat16)
    every = jnp.broadcast_to(mean[None], (groups, rows, BLOCK))
    every = lax.all_to_all(every, "group", split_axis=0, concat_axis=0, tiled=True)
    every = jnp.broadcast_to(every[None], (members, groups, rows, BLOCK))
    every = lax.all_to_all(every, "dev", split_axis=0, concat_axis=0, tiled=True)
    every = every.swapaxes(1, 2).reshape(members * rows, width)
    return (total.astype(jnp.bfloat16), every)


def body(x_act, cotangent, sign_bits):
    rotated, early, late, inexact = fast(x_act, cotangent, sign_bits)
    rotated, mean = assemble(early, late, rotated)
    _, rotated, mean = lax.while_loop(
        lambda state: state[0] > 0.0,
        lambda state: (jnp.float32(0.0), *general(x_act, cotangent, sign_bits)),
        (inexact[0, 0], rotated, mean),
    )
    return rotated, mean


def solution(mesh):
    placed = (P(("group", "dev"), None), P(("group", "dev"), None), P())
    return jax.shard_map(
        body, mesh=mesh, in_specs=placed, out_specs=(P("dev", "group"), P()), check_vma=False
    )
```

```python
import functools

import jax
import jax.numpy as jnp
from jax import lax
from jax.experimental import pallas as pl
from jax.experimental.pallas import tpu as pltpu
from jax.sharding import PartitionSpec as P

BLOCK = 128
TOK = 320
D = 4608
KVW = 1024
STAGES = 9
QUAD = 1152
OWN = 288
PART = 96
SHARE = 32
LAG_A, LAG_B, LAG_C, LAG_D = 1, 4, 8, 11
MAGIC = 12582912.0
MESH = pl.DeviceIdType.MESH
GATHERS = (("xyz", 0, 64), ("yzx", 64, 64), ("zxy", 128, 64), ("xyz", 192, 32), ("yzx", 224, 32), ("zxy", 256, 32))


def hadamard_in_kernel():
    i = lax.broadcasted_iota(jnp.int32, (BLOCK, BLOCK), 0)
    j = lax.broadcasted_iota(jnp.int32, (BLOCK, BLOCK), 1)
    both = i & j
    parity = jnp.zeros_like(both)
    for bit in range(7):
        parity = parity + ((both >> bit) & 1)
    return (1 - 2 * (parity & 1)).astype(jnp.float32).astype(jnp.bfloat16)


def scale_of(largest):
    scale = jnp.full_like(largest, 2.0**-8)
    for e in (32, 16, 8, 4, 2, 1):
        cand = scale * 2.0**e
        scale = jnp.where(largest > cand * 63.5, cand, scale)
    return jnp.minimum(scale, 2.0**30)


def rounded(value, scale):
    shift = scale * MAGIC
    return (value + shift) - shift


def inverse_of(power):
    scale = jnp.full_like(power, 2.0**-8)
    inv = jnp.full_like(power, 2.0**8)
    for e in (32, 16, 8, 4, 2, 1):
        cand = scale * 2.0**e
        take = power >= cand
        scale = jnp.where(take, cand, scale)
        inv = jnp.where(take, inv * 2.0**-e, inv)
    return inv


def on_wire(unit, total):
    inv = inverse_of(unit)
    exact = total * inv * 127.0 <= 32767.0
    return inv, jnp.where(exact, unit, jnp.nan), jnp.where(exact, total, jnp.nan)


def kernel(
    x_hbm, cot_hbm, sb_ref, rot_ref, early, late, bad_ref,
    xv, ct3, tmp0, tmp1, tmp2, tmp3, own, out_, got, om, sm, gm, pw, acc, accm,
    z1, z1m, z1r, z1rm, z2, z2m, z2r, z2rm, xs, xsm, xr, xrm, gbuf, parts, rbuf, rgot, gauge, cot_ref,
    sib_s, sib_r, z1_s, z1_r, z2_s, z2_r, x_s, x_r, g_s, g_r, r_s, r_r, a_s, a_r, f_r, l_s,
):
    g = lax.axis_index("group")
    d = lax.axis_index("dev")
    div, rem = (lambda a, b: lax.div(a, jnp.int32(b))), (lambda a, b: lax.rem(a, jnp.int32(b)))
    xl, y = div(g, 4), rem(g, 4)
    xh, z, c = div(d, 8), rem(div(d, 2), 4), rem(d, 2)
    z_hi, k = div(z, 2), rem(z, 2) * 2 + c
    x = xh * 2 + xl

    def dev(xx, yy, zz, cc):
        return (rem(xx, 2) * 4 + yy, div(xx, 2) * 8 + zz * 2 + cc)

    sibling = dev(x, y, z, 1 - c)
    partner = dev((x + 2) % 4, y, z, c)
    beside = (dev(x, y, (z + 1) % 4, c), dev(x, y, (z + 3) % 4, c))
    column = 2 * k + g // 4
    to_self = jnp.logical_and(k == g // 2, g % 2 == g // 4).astype(jnp.int32)

    fetch_cot = pltpu.make_async_copy(cot_hbm, cot_ref, l_s.at[0])
    fetch_cot.start()
    fetch = pltpu.make_async_copy(x_hbm, xv, l_s.at[1])
    fetch.start()

    bar = pltpu.get_barrier_semaphore()

    def greet(who):
        pl.semaphore_signal(bar, inc=1, device_id=who, device_id_type=MESH)

    greet(sibling)
    for delta in (1, 2, 3):
        greet(dev((x + delta) % 4, y, z, c))
        greet(dev(x, (y + delta) % 4, z, c))
        greet(dev(x, y, (z + delta) % 4, c))
    for delta in (1, 2, 3):
        greet(dev(xh * 2 + 1 - xl, (y + delta) % 4, z, c))
    ksrc = g // 2
    for m in range(4):

        @pl.when(jnp.logical_or(to_self == 0, m != g % 4))
        def _():
            greet(((g % 2) * 4 + m, xh * 8 + (z_hi * 2 + ksrc // 2) * 2 + ksrc % 2))

    hmat = hadamard_in_kernel()
    signs = (2 * sb_ref[...] - 1).astype(jnp.float32)
    fetch_cot.wait()
    for blk in range(8):
        cols = slice(blk * BLOCK, (blk + 1) * BLOCK)
        signed = (cot_ref[:, cols].astype(jnp.float32) * signs[:, cols]).astype(jnp.bfloat16)
        turned = lax.dot_general(hmat, signed, (((1,), (1,)), ((), ())), preferred_element_type=jnp.float32)
        hi = turned.astype(jnp.bfloat16)
        rest = turned - hi.astype(jnp.float32)
        mid = rest.astype(jnp.bfloat16)
        low = (rest - mid.astype(jnp.float32)).astype(jnp.bfloat16)
        kk, b = blk // 2, blk % 2
        r0 = (kk % 2) * 512 + (kk // 2) * 256 + b * BLOCK
        rows = slice(r0, r0 + BLOCK)
        for n, term in enumerate((hi, mid, low)):
            ct3[rows, n * 256 : (n + 1) * 256] = term[:, :256]
        ct3[rows, 768:896] = jnp.concatenate([hi[:, 256:], mid[:, 256:]], axis=1)
        ct3[rows, 896:1024] = jnp.concatenate([low[:, 256:], jnp.zeros((BLOCK, 64), jnp.bfloat16)], axis=1)

    def product(s, core, X, tmp):
        lanes = [pl.ds(pl.multiple_of(X * 2304 + h * QUAD + s * BLOCK, BLOCK), BLOCK) for h in (0, 1)]
        xa = jnp.concatenate([xv[:, l] for l in lanes], axis=1)
        x3 = jnp.concatenate([xa[:256]] * 3 + [xa[256:]] * 3 + [jnp.zeros((64, 256), jnp.bfloat16)], axis=0)
        lhs = ct3[pl.ds(pl.multiple_of(core * 512, 512), 512), :]
        tmp[...] = jnp.dot(lhs, x3, preferred_element_type=jnp.float32)

    def quantized(s, X, tmp, lev, met):
        def sub(Z, b):
            r0, l0 = (Z % 2) * 256 + b * BLOCK, (Z // 2) * BLOCK
            return tmp[r0 : r0 + BLOCK, l0 : l0 + BLOCK]

        largest = jnp.concatenate(
            [jnp.max(jnp.abs(sub(Z, b)), axis=0, keepdims=True) for Z in range(4) for b in range(2)], axis=0
        )
        scale = scale_of(largest)
        met[s, X] = scale
        for Z in range(4):
            for b in range(2):
                r = Z * 2 + b
                lev[s, X, Z, half(b), :] = rounded(sub(Z, b), scale[r : r + 1]).astype(jnp.bfloat16)

    def half(b):
        return slice(b * BLOCK, (b + 1) * BLOCK)

    def remote(src, dst, ss, rs, who):
        return pltpu.make_async_remote_copy(src, dst, ss, rs, device_id=who, device_id_type=MESH)

    def both(src, srcm, dst, dstm, ss, n, rs, who):
        return (remote(src, dst, ss.at[2 * n], rs, who), remote(srcm, dstm, ss.at[2 * n + 1], rs, who))

    def sib_copies(s):
        return both(out_.at[s], sm.at[s], got.at[s], gm.at[s], sib_s, 0, sib_r.at[s], sibling)

    def z1_copies(s, way, n):
        a, b = z1.at[s, way], z1r.at[s, way]
        if n == 1:
            a, b = a.at[0], b.at[0]
        return both(a, z1m.at[s, way], b, z1rm.at[s, way], z1_s, n - 1, z1_r.at[s, way], beside[way])

    def z2_copies(s, way, n):
        a, b = z2.at[s, way], z2r.at[s, way]
        if n == 1:
            a, b = a.at[0], b.at[0]
        return both(a, z2m.at[s, way], b, z2rm.at[s, way], z2_s, n - 1, z2_r.at[s, way], beside[way])

    def x_copies(s, n):
        a, am, b, bm = xs.at[s], xsm.at[s], xr.at[s], xrm.at[s]
        if n == 1:
            a, am, b, bm = a.at[0], am.at[0], b.at[0], bm.at[0]
        return both(a, am, b, bm, x_s, 0 if n == 1 else 1, x_r.at[s], partner)

    def took(sem, rows):
        ref = gauge.at[pl.ds(0, rows), :]
        pltpu.make_async_copy(ref, ref, sem).wait()

    def g_copy(p, q):
        to = rem(g + q, 8)
        three = pl.ds(pl.multiple_of(p * PART, PART), PART)
        return remote(gbuf.at[to, three, :], parts.at[g, three, :], g_s, g_r.at[p], (to, d))

    def r_copy(s):
        t = 4 * s + rem(g, 4)
        j = div(t, 9)
        src = rbuf.at[pl.ds(pl.multiple_of(s * SHARE, SHARE), SHARE), :]
        dst = rgot.at[pl.ds(pl.multiple_of(rem(t, 9) * SHARE, SHARE), SHARE), :]
        who = (column, xh * 8 + (z_hi * 2 + div(j, 2)) * 2 + rem(j, 2))
        return remote(src, dst, r_s.at[s], r_r.at[rem(t, 9)], who), jnp.logical_and(to_self == 1, j == k), t

    def start(copies):
        for copy in copies:
            copy.start()

    def encode(value, inv):
        return (value * inv).astype(jnp.int16)

    def pair_block(s, X, Z, b):
        return own[s, X, Z, half(b), :].astype(jnp.float32) + got[s, X, Z, half(b), :].astype(jnp.float32)

    def add(s, i, b, block, unit, total):
        acc[s, i, half(b), :] = acc[s, i, half(b), :] + block.astype(jnp.float32) * unit
        accm[s, i, b : b + 1, :] = jnp.minimum(accm[s, i, b : b + 1, :], unit)
        accm[s, i, 2 + b : 3 + b, :] = accm[s, i, 2 + b : 3 + b, :] + total

    def packed(s, i, b):
        inv, unit, total = on_wire(accm[s, i, b : b + 1, :], accm[s, i, 2 + b : 3 + b, :])
        return encode(acc[s, i, half(b), :], inv), unit, total

    def z1_from_sums(s):
        two = (z + 2) % 4
        for way, (near, b) in enumerate((((z + 1) % 4, 1), ((z + 3) % 4, 0))):
            for kind, (i, bb) in enumerate(((near, b), (two, 1 - b))):
                block, unit, total = packed(s, i, bb)
                z1[s, way, 0, kind] = block
                z1m[s, way, kind : kind + 1, :] = unit
                z1m[s, way, 2 + kind : 3 + kind, :] = total
            start(z1_copies(s, way, 1))

    def z1_take(s, n, mine, right, left_):
        for way in (0, 1):
            took(z1_r.at[s, way], 256 * n + 16)
            for i in range(n):
                r = 4 * i
                b = way
                on = right(i) if way == 0 else left_(i)
                add(s, on, b, z1r[s, way, i, 1], z1rm[s, way, r + 1 : r + 2, :], z1rm[s, way, r + 3 : r + 4, :])
                block, unit, total = packed(s, on, b)
                z2[s, way, i] = block
                z2m[s, way, i : i + 1, :] = unit
                z2m[s, way, 2 + i : 3 + i, :] = total
            start(z2_copies(s, way, n))
            for i in range(n):
                r = 4 * i
                add(s, mine(i), 1 - way, z1r[s, way, i, 0], z1rm[s, way, r : r + 1, :], z1rm[s, way, r + 2 : r + 3, :])

    def z2_take(s, n, mine):
        for way in (0, 1):
            took(z2_r.at[s, way], 128 * n + 16)
            for i in range(n):
                add(s, mine(i), way, z2r[s, way, i], z2rm[s, way, i : i + 1, :], z2rm[s, way, 2 + i : 3 + i, :])

    def along_z_first(s):
        return rem(s, 3) != 1

    def step_a(s):
        took(sib_r.at[s], 2080)
        for X in (0, 1):
            unit = jnp.minimum(om[s, X], gm[s, X])
            total = om[s, X] + gm[s, X]
            inv, wire_unit, wire_total = on_wire(unit, total)
            for n, v in enumerate((unit, total, inv, wire_unit, wire_total)):
                pw[X, n] = v

        def row(X, n, Z, b):
            return pw[X, n, pl.ds(2 * Z + b, 1), :]

        def keep(i, ii, X, Z, b):
            acc[s, i, half(ii), :] = pair_block(s, X, Z, b)
            accm[s, i, ii : ii + 1, :] = row(X, 0, Z, b)
            accm[s, i, 2 + ii : 3 + ii, :] = row(X, 1, Z, b)

        @pl.when(along_z_first(s))
        def _():
            two, after, before = (z + 2) % 4, (z + 1) % 4, (z + 3) % 4
            for way, (near, b) in enumerate(((after, 1), (before, 0))):
                for X in (0, 1):
                    for kind, (Z, bb) in enumerate(((near, b), (two, 1 - b))):
                        z1[s, way, X, kind] = encode(pair_block(s, X, Z, bb), row(X, 2, Z, bb))
                        z1m[s, way, 4 * X + kind : 4 * X + kind + 1, :] = row(X, 3, Z, bb)
                        z1m[s, way, 4 * X + 2 + kind : 4 * X + 3 + kind, :] = row(X, 4, Z, bb)
                start(z1_copies(s, way, 2))
            for X in (0, 1):
                for b in (0, 1):
                    keep(X, b, X, z, b)
                keep(2 + X, 0, X, after, 0)
                keep(2 + X, 1, X, before, 1)

        @pl.when(jnp.logical_not(along_z_first(s)))
        def _():
            for Z in range(4):
                for b in (0, 1):
                    xs[s, Z, half(b), :] = encode(pair_block(s, 1 - xh, Z, b), row(1 - xh, 2, Z, b))
                    xsm[s, Z, b : b + 1, :] = row(1 - xh, 3, Z, b)
                    xsm[s, Z, 2 + b : 3 + b, :] = row(1 - xh, 4, Z, b)
            start(x_copies(s, 4))
            for Z in range(4):
                for b in (0, 1):
                    keep(Z, b, xh, Z, b)

    def x_take(s, i, n):
        for b in (0, 1):
            add(s, i, b, xr[s, n, half(b), :], xrm[s, n, b : b + 1, :], xrm[s, n, 2 + b : 3 + b, :])

    def step_b(s):
        @pl.when(along_z_first(s))
        def _():
            z1_take(s, 2, lambda i: i, lambda i: 2 + i, lambda i: 2 + i)

        @pl.when(jnp.logical_not(along_z_first(s)))
        def _():
            took(x_r.at[s], 1088)
            for Z in range(4):
                x_take(s, Z, Z)
            z1_from_sums(s)

    def step_c(s):
        @pl.when(along_z_first(s))
        def _():
            z2_take(s, 2, lambda i: i)
            for b in (0, 1):
                block, unit, total = packed(s, 1 - xh, b)
                xs[s, 0, half(b), :] = block
                xsm[s, 0, b : b + 1, :] = unit
                xsm[s, 0, 2 + b : 3 + b, :] = total
            start(x_copies(s, 1))

        @pl.when(jnp.logical_not(along_z_first(s)))
        def _():
            z1_take(s, 1, lambda i: z, lambda i: (z + 1) % 4, lambda i: (z + 3) % 4)

    def step_d(s):
        @pl.when(along_z_first(s))
        def _():
            took(x_r.at[s], 272)
            x_take(s, xh, 0)

        @pl.when(jnp.logical_not(along_z_first(s)))
        def _():
            z2_take(s, 1, lambda i: z)

        i = jnp.where(along_z_first(s), xh, z)
        sums = [acc[s, i, half(b), :] for b in (0, 1)]
        largest = jnp.concatenate([jnp.max(jnp.abs(t), axis=0, keepdims=True) for t in sums], axis=0)
        scale = scale_of(largest)
        for b in (0, 1):
            value = rounded(sums[b], scale[b : b + 1])
            value = value.T.astype(jnp.bfloat16)
            for m in range(4):
                gbuf[4 * b + m, pl.ds(pl.multiple_of(s * SHARE, SHARE), SHARE), :] = value[m * SHARE : (m + 1) * SHARE]

        @pl.when(rem(s, 3) == 2)
        def _():
            for q in range(1, 8):
                g_copy(div(s, 3), q).start()

    def moved(axis, delta):
        return (
            rem(x + delta, 4) if axis == "x" else x,
            rem(y + delta, 4) if axis == "y" else y,
            rem(z + delta, 4) if axis == "z" else z,
        )

    def mine(j, n):
        return {"x": x, "y": y, "z": z}[GATHERS[j][0][n]]

    def held(j, core, *index):
        ref, n = (early, j) if j < 3 else (late, j - 3)
        return ref.at[(n, core) + index]

    def to_mate(j, phase, delta, ref, n):
        who = dev(*moved(GATHERS[j][0][phase], delta), c)
        return remote(ref, ref, a_s.at[j, phase], a_r.at[j, n], who)

    def half_slab(j, ring, h):
        return held(j, c, rem(mine(j, 2) + ring, 4), pl.ds(2 * h, 2))

    def last(j, way, h, ring, n):
        to_mate(j, 2, way, half_slab(j, ring, h), n).start()

    def forward(j, ring):
        ref = held(j, c, rem(mine(j, 2) + ring, 4))
        remote(ref, ref, a_s.at[j, 3], f_r.at[j], sibling).start()

    def phase0(j, mean):
        block = held(j, c, mine(j, 2), mine(j, 1), mine(j, 0))
        block[...] = mean
        for delta in (1, 3, 2):
            to_mate(j, 0, delta, block, 0).start()

    def phase1(j):
        took(a_r.at[j, 0], 3 * GATHERS[j][2])
        for delta in (1, 3, 2):
            to_mate(j, 1, delta, held(j, c, mine(j, 2), mine(j, 1)), 1).start()

    def phase2(j):
        took(a_r.at[j, 1], 12 * GATHERS[j][2])
        last(j, 1, 0, 0, 2)
        last(j, 3, 1, 0, 3)
        last(j, 1, 1, 0, 4)
        last(j, 3, 0, 0, 4)
        forward(j, 0)

    def relay(j):
        took(a_r.at[j, 2], 8 * GATHERS[j][2])
        last(j, 1, 0, 3, 5)
        took(a_r.at[j, 3], 8 * GATHERS[j][2])
        last(j, 3, 1, 1, 5)

    def spread(j):
        took(a_r.at[j, 4], 16 * GATHERS[j][2])
        forward(j, 3)
        forward(j, 1)

    def finish(j):
        took(a_r.at[j, 5], 16 * GATHERS[j][2])
        forward(j, 2)

    fetch.wait()

    def loop(t, _):
        @pl.when(t < STAGES)
        def _():
            product(t, 1 - c, 0, tmp0)
            product(t, 1 - c, 1, tmp1)
            quantized(t, 0, tmp0, out_, sm)
            product(t, c, 0, tmp2)
            quantized(t, 1, tmp1, out_, sm)
            product(t, c, 1, tmp3)

            @pl.when(t == 0)
            def _():
                pl.semaphore_wait(bar, 17 - to_self)

            start(sib_copies(t))
            quantized(t, 0, tmp2, own, om)
            quantized(t, 1, tmp3, own, om)

        for lag, step in ((LAG_A, step_a), (LAG_B, step_b), (LAG_C, step_c), (LAG_D, step_d)):

            @pl.when(jnp.logical_and(t >= lag, t < STAGES + lag))
            def _():
                step(t - lag)

        return 0

    lax.fori_loop(0, STAGES + LAG_D, loop, 0)

    my_signs = (2 * sb_ref[:, pl.ds(pl.multiple_of(column * BLOCK, BLOCK), BLOCK)] - 1).astype(jnp.float32)
    parts[g] = gbuf[g]

    def chain(first, end, bad):
        total = parts[0, first:end, :].astype(jnp.float32)
        for other in range(1, 8):
            total = total + parts[other, first:end, :].astype(jnp.float32)
            total = rounded(total, scale_of(jnp.max(jnp.abs(total), axis=1, keepdims=True)))
        total = total * (1.0 / 128.0)
        rbuf[first:end, :] = total.astype(jnp.bfloat16)
        turned = jnp.dot(total.astype(jnp.bfloat16), hmat, preferred_element_type=jnp.float32)
        mean = turned * (1.0 / BLOCK) * my_signs
        bad = jnp.maximum(bad, jnp.max(jnp.where(mean == mean, 0.0, 1.0), axis=(0, 1), keepdims=True))
        return jnp.where(bad > 0.0, jnp.nan, mean).astype(jnp.bfloat16), bad

    bad = jnp.zeros((1, 1), jnp.float32)
    for arrived, first, end, gathers in (((0, 1), 0, 2 * PART, (0, 1, 2)), ((2,), 2 * PART, OWN, (3, 4, 5))):
        for p in arrived:
            took(g_r.at[p], 7 * PART)
        mean, bad = chain(first, end, bad)
        for j in gathers:
            _, row, rows = GATHERS[j]
            phase0(j, mean[row - first : row - first + rows])
    for j in range(6):
        phase1(j)

    for j in range(6):
        phase2(j)

    def send_rotated(s, _):
        copy, here, t = r_copy(s)

        @pl.when(here)
        def _():
            rgot[pl.ds(pl.multiple_of(rem(t, 9) * SHARE, SHARE), SHARE), :] = rbuf[
                pl.ds(pl.multiple_of(s * SHARE, SHARE), SHARE), :
            ]

        @pl.when(jnp.logical_not(here))
        def _():
            copy.start()

        return 0

    lax.fori_loop(0, STAGES, send_rotated, 0)
    for ref, sem in (
        (out_, sib_s.at[0]), (sm, sib_s.at[1]),
        (z1.at[0:3, :, 0], z1_s.at[0]), (z1m.at[0:3], z1_s.at[1]), (z1.at[0:6], z1_s.at[2]), (z1m.at[0:6], z1_s.at[3]),
        (z2.at[0:3, :, 0], z2_s.at[0]), (z2m.at[0:3], z2_s.at[1]), (z2.at[0:6], z2_s.at[2]), (z2m.at[0:6], z2_s.at[3]),
        (xs.at[0:6, 0], x_s.at[0]), (xsm.at[0:6, 0], x_s.at[1]), (xs.at[0:3], x_s.at[2]), (xsm.at[0:3], x_s.at[3]),
        (gbuf.at[0:7], g_s),
    ):
        pltpu.make_async_copy(ref, ref, sem).wait()
    for j in range(3):
        relay(j)
    for j in range(3):
        spread(j)
    for j in range(3, 6):
        relay(j)
    for j in range(3, 6):
        spread(j)

    def drain_rotated(u, _):
        t = 9 * k + u

        @pl.when(jnp.logical_or(to_self == 0, rem(t, 4) != rem(g, 4)))
        def _():
            ref = rgot.at[pl.ds(pl.multiple_of(u * SHARE, SHARE), SHARE), :]
            remote(ref, ref, r_s.at[u], r_r.at[u], sibling).wait_recv()

        copy, here, _ = r_copy(u)

        @pl.when(jnp.logical_not(here))
        def _():
            copy.wait_send()

        return 0

    lax.fori_loop(0, STAGES, drain_rotated, 0)
    rot_ref[...] = rgot[...]
    for j in range(6):
        finish(j)
    for j in range(6):
        took(f_r.at[j], 64 * GATHERS[j][2])
    for j in range(6):
        for n, blocks in enumerate((3, 12, 48, 64)):
            took(a_s.at[j, n], blocks * GATHERS[j][2])
    marks = jnp.zeros((16, BLOCK), jnp.float32)
    for core in range(2):
        for i in range(4):
            for j in range(4):
                for n in range(4):
                    marks = marks + late[2, core, i, j, n, 0:16, :].astype(jnp.float32)
    bad_ref[0, 0] = jnp.max(jnp.where(marks == marks, 0.0, 1.0))


def fast(x_act, cotangent, sign_bits):
    bf16, f32, i16 = jnp.bfloat16, jnp.float32, jnp.int16
    dma = pltpu.SemaphoreType.DMA
    vmem = pltpu.VMEM
    return pl.pallas_call(
        kernel,
        out_shape=(
            vmem((OWN, BLOCK), bf16),
            vmem((3, 2, 4, 4, 4, 2 * SHARE, BLOCK), bf16),
            vmem((3, 2, 4, 4, 4, SHARE, BLOCK), bf16),
            jax.ShapeDtypeStruct((1, 1), f32),
        ),
        in_specs=[pl.BlockSpec(memory_space=pl.ANY)] * 2 + [pl.BlockSpec(memory_space=vmem)],
        out_specs=(
            pl.BlockSpec(memory_space=vmem),
            pl.BlockSpec(memory_space=vmem),
            pl.BlockSpec(memory_space=vmem),
            pl.BlockSpec(memory_space=pltpu.SMEM),
        ),
        scratch_shapes=[
            vmem((TOK, D), bf16),
            vmem((KVW, KVW), bf16),
            vmem((512, 256), f32), vmem((512, 256), f32), vmem((512, 256), f32), vmem((512, 256), f32),
            vmem((STAGES, 2, 4, 256, BLOCK), bf16),
            vmem((STAGES, 2, 4, 256, BLOCK), bf16),
            vmem((STAGES, 2, 4, 256, BLOCK), bf16),
            vmem((STAGES, 2, 8, BLOCK), f32),
            vmem((STAGES, 2, 8, BLOCK), f32),
            vmem((STAGES, 2, 8, BLOCK), f32),
            vmem((2, 5, 8, BLOCK), f32),
            vmem((STAGES, 4, 256, BLOCK), f32),
            vmem((STAGES, 4, 8, BLOCK), f32),
            vmem((STAGES, 2, 2, 2, BLOCK, BLOCK), i16),
            vmem((STAGES, 2, 8, BLOCK), f32),
            vmem((STAGES, 2, 2, 2, BLOCK, BLOCK), i16),
            vmem((STAGES, 2, 8, BLOCK), f32),
            vmem((STAGES, 2, 2, BLOCK, BLOCK), i16),
            vmem((STAGES, 2, 8, BLOCK), f32),
            vmem((STAGES, 2, 2, BLOCK, BLOCK), i16),
            vmem((STAGES, 2, 8, BLOCK), f32),
            vmem((STAGES, 4, 256, BLOCK), i16),
            vmem((STAGES, 4, 8, BLOCK), f32),
            vmem((STAGES, 4, 256, BLOCK), i16),
            vmem((STAGES, 4, 8, BLOCK), f32),
            vmem((8, OWN, BLOCK), bf16),
            vmem((8, OWN, BLOCK), bf16),
            vmem((OWN, BLOCK), bf16),
            vmem((OWN, BLOCK), bf16),
            vmem((64 * PART, BLOCK), bf16),
            vmem((TOK, KVW), bf16),
            dma((2,)), dma((STAGES,)),
            dma((4,)), dma((STAGES, 2)),
            dma((4,)), dma((STAGES, 2)),
            dma((4,)), dma((STAGES,)),
            dma, dma((3,)),
            dma((STAGES,)), dma((STAGES,)),
            dma((6, 4)), dma((6, 6)),
            dma((6,)), dma((2,)),
        ],
        compiler_params=pltpu.CompilerParams(
            collective_id=0, has_side_effects=True, vmem_limit_bytes=53 * 2**20
        ),
        cost_estimate=pl.CostEstimate(flops=10**10, bytes_accessed=3 * 10**7, transcendentals=0),
        name="sync",
    )(x_act, cotangent, sign_bits.reshape(1, KVW))


def assemble_kernel(early, late, rot_ref, rot_out, out_hbm, rows, sems):
    rot_out[...] = rot_ref[...]
    copies = []
    for quad in range(4):
        for s in range(STAGES):
            n = quad * STAGES + s
            for k in range(4):
                for g in range(8):
                    xh, z, c = quad // 2, (quad % 2) * 2 + k // 2, k % 2
                    x, y = xh * 2 + g // 4, g % 4
                    ref, j, r = (early, s // 2, s % 2 * SHARE) if s < 6 else (late, s - 6, 0)
                    axes = GATHERS[j if s < 6 else j + 3][0]
                    where = tuple({"x": x, "y": y, "z": z}[axes[n_axis]] for n_axis in (2, 1, 0))
                    column = 2 * k + g // 4
                    rows[
                        n, y * SHARE : (y + 1) * SHARE, column * BLOCK : (column + 1) * BLOCK
                    ] = ref[(j, c) + where + (slice(r, r + SHARE),)]
            copies.append(
                pltpu.make_async_copy(rows.at[n], out_hbm.at[pl.ds(n * BLOCK, BLOCK), :], sems.at[n])
            )
            copies[-1].start()
    for copy in copies:
        copy.wait()


def assemble(early, late, rotated):
    vmem = pl.BlockSpec(memory_space=pltpu.VMEM)
    return pl.pallas_call(
        assemble_kernel,
        out_shape=(
            jax.ShapeDtypeStruct((OWN, BLOCK), jnp.bfloat16),
            jax.ShapeDtypeStruct((D, KVW), jnp.bfloat16),
        ),
        in_specs=[vmem, vmem, vmem],
        out_specs=(vmem, pl.BlockSpec(memory_space=pl.ANY)),
        scratch_shapes=[
            pltpu.VMEM((4 * STAGES, BLOCK, KVW), jnp.bfloat16),
            pltpu.SemaphoreType.DMA((4 * STAGES,)),
        ],
        compiler_params=pltpu.CompilerParams(vmem_limit_bytes=24 * 2**20),
        cost_estimate=pl.CostEstimate(flops=0, bytes_accessed=2 * 10**7, transcendentals=0),
        name="assemble",
    )(early, late, rotated)


def hadamard():
    index_vals = jnp.arange(BLOCK)
    both = jnp.bitwise_and(index_vals[:, None], index_vals[None, :])
    parity = jnp.zeros_like(both)
    for bit_pos in range(7):
        parity = parity + jnp.bitwise_and(jnp.right_shift(both, bit_pos), 1)
    return (1 - 2 * (parity % 2)).astype(jnp.float32)


def rotate(matrix, signs, hmat):
    rows = matrix.shape[0]
    blocks = (matrix * signs[None, :]).reshape(rows, -1, BLOCK)
    turned = jnp.einsum("rbi,ij->rbj", blocks, hmat, precision=lax.Precision.HIGHEST)
    return turned.reshape(rows, -1)


def unrotate(matrix, signs, hmat):
    rows = matrix.shape[0]
    blocks = matrix.reshape(rows, -1, BLOCK)
    turned = jnp.einsum("rbi,ij->rbj", blocks, hmat, precision=lax.Precision.HIGHEST)
    return (turned / BLOCK).reshape(rows, -1) * signs[None, :]


def quantize(matrix):
    shape = matrix.shape
    blocks = matrix.reshape(shape[:-1] + (shape[-1] // BLOCK, BLOCK))
    largest = jnp.max(jnp.abs(blocks), axis=-1)
    powers = jnp.asarray([2.0**k for k in range(-7, 31)], dtype=jnp.float32)
    exceeds = largest[..., None] > 63.5 * powers
    scales = jnp.max(jnp.where(exceeds, powers, 0.00390625), axis=-1).astype(jnp.bfloat16)
    ratio = blocks / scales.astype(jnp.float32)[..., None]
    floored = jnp.floor(ratio)
    fraction = ratio - floored
    odd_level = floored - 2.0 * jnp.floor(0.5 * floored) == 1.0
    round_up = (fraction > 0.5) | (fraction == 0.5) & odd_level
    levels = (floored + round_up.astype(jnp.float32)).astype(jnp.bfloat16)
    return (levels.reshape(shape), scales)


def dequant(levels, scales):
    shape = levels.shape
    blocks = levels.astype(jnp.float32).reshape(shape[:-1] + (shape[-1] // BLOCK, BLOCK))
    return (blocks * scales.astype(jnp.float32)[..., None]).reshape(shape)


def general(x_act, cotangent, sign_bits):
    signs = (2 * sign_bits - 1).astype(jnp.float32)
    hmat = hadamard()
    local = lax.dot_general(
        x_act, cotangent, (((0,), (0,)), ((), ())), preferred_element_type=jnp.float32
    )
    levels, scales = quantize(rotate(local, signs, hmat))
    width = levels.shape[1]
    members = lax.axis_size("dev")
    groups = lax.axis_size("group")
    rows = levels.shape[0] // members
    got_levels, got_scales = (
        lax.all_to_all(
            levels.reshape(members, rows, width), "dev", split_axis=0, concat_axis=0, tiled=True
        ),
        lax.all_to_all(
            scales.reshape(members, rows, width // BLOCK),
            "dev",
            split_axis=0,
            concat_axis=0,
            tiled=True,
        ),
    )
    group_total = jnp.sum(dequant(got_levels, got_scales), axis=0)
    part = dequant(*quantize(group_total)).astype(jnp.bfloat16)
    blocks = part.reshape(rows, groups, BLOCK).swapaxes(0, 1)
    arrived = lax.all_to_all(blocks, "group", split_axis=0, concat_axis=0, tiled=True).astype(jnp.float32)
    running = arrived[0]
    for other in range(1, groups):
        running = dequant(*quantize(running + arrived[other]))
    total = running / (groups * members)
    position = lax.axis_index("group")
    my_signs = lax.dynamic_slice_in_dim(signs, position * BLOCK, BLOCK, 0)
    mean = unrotate(total, my_signs, hmat).astype(jnp.bfloat16)
    every = jnp.broadcast_to(mean[None], (groups, rows, BLOCK))
    every = lax.all_to_all(every, "group", split_axis=0, concat_axis=0, tiled=True)
    every = jnp.broadcast_to(every[None], (members, groups, rows, BLOCK))
    every = lax.all_to_all(every, "dev", split_axis=0, concat_axis=0, tiled=True)
    every = every.swapaxes(1, 2).reshape(members * rows, width)
    return (total.astype(jnp.bfloat16), every)


def body(x_act, cotangent, sign_bits):
    rotated, early, late, inexact = fast(x_act, cotangent, sign_bits)
    rotated, mean = assemble(early, late, rotated)
    _, rotated, mean = lax.while_loop(
        lambda state: state[0] > 0.0,
        lambda state: (jnp.float32(0.0), *general(x_act, cotangent, sign_bits)),
        (inexact[0, 0], rotated, mean),
    )
    return rotated, mean


def solution(mesh):
    placed = (P(("group", "dev"), None), P(("group", "dev"), None), P())
    return jax.shard_map(
        body, mesh=mesh, in_specs=placed, out_specs=(P("dev", "group"), P()), check_vma=False
    )
```
